1024 devices in a mesh: img: 128 (over y_lo, z, x), dp: 8 (over y_hi, core).
Axes of the slice: x: 4, y: 8 (y_hi: 4, y_lo: 2; y = y_hi * 2 + y_lo), z: 16, core: 2. Of those that a mesh axis runs over, the one named last changes fastest.
Arguments:
- image_feats: bfloat16 [8, 24576, 1152], P('dp', 'img'), may hold values from -6 to 6
- text_feats: bfloat16 [8, 24576, 1152], P('dp', 'img'), may hold values from -6 to 6
- gains: float32 [2, 1152], replicated, may hold values from 0.5 to 1.5
- shifts: float32 [2, 1152], replicated, may hold values from -1 to 1
- log_scale: float32 [1], replicated, may hold values from 3 to 4
- logit_bias: float32 [1], replicated, may hold values from -3 to -1
Outputs:
- image_grad: bfloat16 [8, 24576, 1152], P('dp', 'img')
- text_grad: bfloat16 [8, 24576, 1152], P('dp', 'img')
- gain_grads: float32 [2, 1152], replicated
- shift_grads: float32 [2, 1152], replicated
- row_loss: float32 [8, 24576], P('dp', 'img')
The draws below stay inside these ranges and needn't reach their ends.
All inputs are finite; a program needn't handle non-finite values.
Results may differ from the reference program's by a relative error of at most 0.0036.
Values may be sent and summed in bfloat16 or wider, within the bound.
No kernel may reach another device: no remote copies, remote signals or barrier semaphores. Data moves between devices by JAX's collectives and lax.ppermute only.
A program may use at most 32 MiB of HBM per device.

```python
import jax
import jax.numpy as jnp
from jax import lax

E = 1152
B_DEV = 192
GROUP_DEVS = 8
GROUP = 1536
ROWS = 24576
N_IMG = 128
N_DP = 8


def level_of(own_key, extent, pieces, low, top_value):
    factor_of, own = 1.0, jax.random.fold_in(own_key, 6)
    for axis_at, shards_of in pieces:
        draws = jnp.exp(jax.random.uniform(jax.random.fold_in(own, axis_at), (shards_of,), jnp.float32, low / len(pieces), top_value / len(pieces)))
        factor_of = factor_of * jnp.repeat(draws, extent[axis_at] // shards_of).reshape([-1 if axis == axis_at else 1 for axis in range(len(extent))])
    return factor_of


def gaussian(key, extent, deviation, bound, cuts=(), kind=jnp.bfloat16):
    values = jax.random.normal(key, extent, jnp.float32) * deviation
    if len(cuts) > 0:
        values = level_of(key, extent, cuts, -0.22, 0.18) * values
    return jnp.clip(values, min=-bound, max=bound).astype(kind)


def setup_inputs(seed: int = 0) -> dict:
    arg_keys = jax.random.split(jax.random.key(seed), 7)
    image_feats = gaussian(arg_keys[0], (N_DP, ROWS, E), 1.0, 6.0, ((0, 8), (1, 128)))
    text_feats = gaussian(arg_keys[1], (N_DP, ROWS, E), 1.0, 6.0, ((0, 8), (1, 128)))
    gains = jnp.clip(1.0 + 0.1 * jax.random.normal(arg_keys[2], (2, E), jnp.float32), 0.5, 1.5)
    shifts = gaussian(arg_keys[3], (2, E), 0.2, 1.0, (), jnp.float32)
    log_scale = jnp.clip(jax.random.uniform(arg_keys[4], (1,), jnp.float32, 3.0, 4.0), 3.0, 4.0)
    logit_bias = jnp.clip(jax.random.uniform(arg_keys[5], (1,), jnp.float32, -3.0, -1.0), -3.0, -1.0)
    return dict(image_feats=image_feats, text_feats=text_feats, gains=gains, shifts=shifts, log_scale=log_scale, logit_bias=logit_bias)


def final_norm(feats, gain_row, shift_row):
    center = lax.optimization_barrier(jnp.mean(feats, axis=-1, keepdims=True))
    offset = feats - center
    spread = lax.optimization_barrier(jnp.mean(offset * offset, axis=-1, keepdims=True))
    normed = offset * lax.rsqrt(spread + 1e-06)
    unnormed = normed * gain_row + shift_row
    return unnormed * lax.rsqrt(lax.optimization_barrier(jnp.sum(unnormed * unnormed, axis=-1, keepdims=True)) + 1e-06)

def one_group(image_rows, text_rows, gains, shifts, logit_scale, logit_shift):
    image_unit, image_pull = jax.vjp(final_norm, image_rows.astype(jnp.float32), gains[0], shifts[0])
    text_unit, text_pull = jax.vjp(final_norm, text_rows.astype(jnp.float32), gains[1], shifts[1])
    image_emb = image_unit.astype(jnp.bfloat16)
    text_emb = text_unit.astype(jnp.bfloat16)
    logits = logit_scale * jnp.dot(image_emb, text_emb.T, preferred_element_type=jnp.float32) + logit_shift
    count = logits.shape[0]
    labels = 2.0 * jnp.eye(count, dtype=jnp.float32) - 1.0
    row_mean = lax.optimization_barrier(jnp.mean(jax.nn.softplus(-labels * logits), axis=1))
    coeff = (-labels * jax.nn.sigmoid(-labels * logits)).astype(jnp.bfloat16)
    image_unit_grad = logit_scale * jnp.dot(coeff, text_emb, preferred_element_type=jnp.float32)
    text_unit_grad = logit_scale * jnp.dot(coeff.T, image_emb, preferred_element_type=jnp.float32)
    image_feat_grad, image_gain, image_shift = image_pull(image_unit_grad)
    text_feat_grad, text_gain, text_shift = text_pull(text_unit_grad)
    gain_part = jnp.stack([image_gain, text_gain])
    shift_part = jnp.stack([image_shift, text_shift])
    return (image_feat_grad.astype(jnp.bfloat16), text_feat_grad.astype(jnp.bfloat16), gain_part, shift_part, row_mean)

def reference(image_feats, text_feats, gains, shifts, log_scale, logit_bias):
    logit_scale = jnp.exp(log_scale[0])
    logit_shift = logit_bias[0]
    stride = N_IMG // GROUP_DEVS

    def regroup(feats):
        shaped = feats.reshape(N_DP, GROUP_DEVS, stride, B_DEV, E).transpose(0, 2, 1, 3, 4)
        return shaped.reshape(N_DP * stride, GROUP, E)

    def ungroup(feats):
        shaped = feats.reshape(N_DP, stride, GROUP_DEVS, B_DEV, E).transpose(0, 2, 1, 3, 4)
        return shaped.reshape(N_DP, ROWS, E)

    def step_group(pair):
        return one_group(pair[0], pair[1], gains, shifts, logit_scale, logit_shift)
    image_grad, text_grad, gain_parts, shift_parts, row_means = lax.map(step_group, (regroup(image_feats), regroup(text_feats)))
    row_loss = row_means.reshape(N_DP, stride, GROUP_DEVS, B_DEV).transpose(0, 2, 1, 3).reshape(N_DP, ROWS)
    return (ungroup(image_grad), ungroup(text_grad), lax.optimization_barrier(jnp.sum(gain_parts, axis=0)), lax.optimization_barrier(jnp.sum(shift_parts, axis=0)), row_loss)
```

```python
import jax
import jax.numpy as jnp
from jax import lax
from jax.sharding import PartitionSpec as P

AXES = ("img", "dp")
RING = 4
X_CHIPS = 4
Z_BLOCK = 4
Y_HIGH = 4


def final_norm(feats, gain_row, shift_row):
    center = jnp.mean(feats, axis=-1, keepdims=True)
    offset = feats - center
    spread = jnp.mean(offset * offset, axis=-1, keepdims=True)
    normed = offset * lax.rsqrt(spread + 1e-06)
    unnormed = normed * gain_row + shift_row
    return unnormed * lax.rsqrt(jnp.sum(unnormed * unnormed, axis=-1, keepdims=True) + 1e-06)


def near(place):
    return place ^ 1


def far(place):
    return RING - 1 - place


class Routes:
    def __init__(self, sizes):
        self.sizes = sizes
        y_lo, z_hi, z_lo, x, y_hi, core = sizes
        self.count = y_lo * z_hi * z_lo * x * y_hi * core

    def split(self, index):
        place = []
        for size in reversed(self.sizes):
            place.append(index % size)
            index //= size
        return place[::-1]

    def join(self, place):
        index = 0
        for size, at in zip(self.sizes, place):
            index = index * size + at
        return index

    def pairs(self, move):
        out = []
        for index in range(self.count):
            place = self.split(index)
            out.append((index, self.join(move(list(place)))))
        return out

    def along(self, axis, step):
        def move(place):
            place[axis] = step(place[axis])
            return place

        return self.pairs(move)

    def across_y(self):
        return self.along(0, near)

    def towers(self):
        def text(place):
            place[1] = far(place[1]) if place[5] == 0 else near(place[1])
            return place

        def image(place):
            place[1] = near(place[1]) if place[5] == 0 else far(place[1])
            return place

        return self.pairs(text), self.pairs(image)

    def everyone(self):
        steps = []
        for axis in (5, 3, 2, 0, 4, 1):
            if self.sizes[axis] >= 2:
                steps.append(self.along(axis, near))
            if self.sizes[axis] == 4:
                steps.append(self.along(axis, far))
        return steps


def send(value, pairs):
    return lax.ppermute(value, AXES, pairs)


def sum_everywhere(value, steps):
    for pairs in steps:
        value = value + send(value, pairs)
    return value


def make_body(routes):
    text_pairs, image_pairs = routes.towers()
    y_pairs = routes.across_y()
    steps = routes.everyone()
    group_rows = 2 * RING

    def body(image_feats, text_feats, gains, shifts, log_scale, logit_bias):
        logit_scale = jnp.exp(log_scale[0])
        logit_shift = logit_bias[0]
        text_unit, text_pull = jax.vjp(
            final_norm, text_feats[0].astype(jnp.float32), gains[1], shifts[1]
        )
        text_emb = text_unit.astype(jnp.bfloat16)
        image_unit, image_pull = jax.vjp(
            final_norm, image_feats[0].astype(jnp.float32), gains[0], shifts[0]
        )
        image_emb = image_unit.astype(jnp.bfloat16)
        rows = image_emb.shape[0]

        text_z = send(text_emb, text_pairs)
        image_z = send(image_emb, image_pairs)
        text_y = send(text_emb, y_pairs)
        text_zy = send(text_z, y_pairs)

        images = jnp.concatenate([image_emb, image_z], axis=0)
        texts = jnp.concatenate([text_emb, text_z, text_y, text_zy], axis=0)
        logits = (
            logit_scale * jnp.dot(images, texts.T, preferred_element_type=jnp.float32)
            + logit_shift
        )
        row_at = lax.broadcasted_iota(jnp.int32, logits.shape, 0)
        column_at = lax.broadcasted_iota(jnp.int32, logits.shape, 1)
        signs = jnp.where((row_at == column_at) & (row_at < rows), -1.0, 1.0)
        loss_sums = jnp.sum(jax.nn.softplus(signs * logits), axis=1)
        coeff = (signs * jax.nn.sigmoid(signs * logits)).astype(jnp.bfloat16)

        text_parts = jnp.dot(coeff.T, images, preferred_element_type=jnp.float32)
        text_zy_back = send(text_parts[3 * rows :].astype(jnp.bfloat16), y_pairs)
        image_parts = jnp.dot(coeff, texts, preferred_element_type=jnp.float32)
        image_back = send(image_parts[rows:].astype(jnp.bfloat16), image_pairs)
        loss_back = send(loss_sums[rows:], image_pairs)
        text_y_back = send(text_parts[2 * rows : 3 * rows].astype(jnp.bfloat16), y_pairs)
        text_z_sum = text_parts[rows : 2 * rows] + text_zy_back.astype(jnp.float32)
        text_z_back = send(text_z_sum.astype(jnp.bfloat16), text_pairs)

        image_acc = image_parts[:rows] + image_back.astype(jnp.float32)
        text_acc = (
            text_parts[:rows] + text_y_back.astype(jnp.float32) + text_z_back.astype(jnp.float32)
        )
        row_mean = (loss_sums[:rows] + loss_back) / (group_rows * rows)

        image_feat_grad, image_gain, image_shift = image_pull(logit_scale * image_acc)
        text_feat_grad, text_gain, text_shift = text_pull(logit_scale * text_acc)
        sums = sum_everywhere(jnp.stack([image_gain, text_gain, image_shift, text_shift]), steps)
        image_grad = image_feat_grad.astype(jnp.bfloat16)[None]
        text_grad = text_feat_grad.astype(jnp.bfloat16)[None]
        return (image_grad, text_grad, sums[:2], sums[2:], row_mean[None])

    return body


def build(mesh, sizes):
    placed = (P("dp", "img", None), P("dp", "img", None), P(), P(), P(), P())
    return jax.shard_map(
        make_body(Routes(sizes)),
        mesh=mesh,
        in_specs=placed,
        out_specs=(P("dp", "img", None), P("dp", "img", None), P(), P(), P("dp", "img")),
        check_vma=False,
    )


def solution(mesh):
    y_high, cores = Y_HIGH, mesh.shape["dp"] // Y_HIGH
    y_low = mesh.shape["img"] // (RING * Z_BLOCK * X_CHIPS)
    return build(mesh, (y_low, RING, Z_BLOCK, X_CHIPS, y_high, cores))
```

```python
import functools

import jax
import jax.numpy as jnp
from jax import lax
from jax.experimental import pallas as pl
from jax.experimental.pallas import tpu as pltpu
from jax.sharding import PartitionSpec as P

AXES = ("img", "dp")
RING = 4
X_CHIPS = 4
Z_BLOCK = 4
Y_HIGH = 4

VMEM_LIMIT = 60 << 20
TILE_VMEM_LIMIT = 24 << 20
ROW_BLOCK = 16
UNROLL = 4
EPS = 1e-06
EXTRA = 16
LANES = 256
NT = (((1,), (1,)), ((), ()))
TN = (((0,), (0,)), ((), ()))


def to_lanes(column):
    count = column.shape[0]
    on = lax.broadcasted_iota(jnp.int32, (count, count), 0) == lax.broadcasted_iota(
        jnp.int32, (count, count), 1
    )
    return jnp.sum(jnp.where(on, column, 0.0), axis=0, keepdims=True)


def to_rows(line):
    count = line.shape[1]
    on = lax.broadcasted_iota(jnp.int32, (count, count), 0) == lax.broadcasted_iota(
        jnp.int32, (count, count), 1
    )
    return jnp.sum(jnp.where(on, line, 0.0), axis=1, keepdims=True)


def put_line(ref, line):
    count = line.shape[1]
    rows = ref.shape[0] - EXTRA
    ref[rows:, :] = jnp.zeros((EXTRA, ref.shape[1]), ref.dtype)
    for term in range(3):
        piece = line.astype(jnp.bfloat16)
        line = line - piece.astype(jnp.float32)
        ref[rows:, term * LANES : term * LANES + count] = jnp.broadcast_to(piece, (EXTRA, count))


def get_line(block, count):
    terms = [
        block[:1, term * LANES : term * LANES + count].astype(jnp.float32) for term in range(3)
    ]
    return terms[0] + (terms[1] + terms[2])


def norm_rows(feats, gain, shift):
    center = jnp.mean(feats, axis=-1, keepdims=True)
    offset = feats - center
    spread = jnp.mean(offset * offset, axis=-1, keepdims=True)
    rstd = lax.rsqrt(spread + EPS)
    normed = offset * rstd
    unnormed = normed * gain + shift
    inverse = lax.rsqrt(jnp.sum(unnormed * unnormed, axis=-1, keepdims=True) + EPS)
    return normed, rstd, unnormed, inverse


def forward_kernel(image_ref, text_ref, gains_ref, shifts_ref, image_emb_ref, text_emb_ref, keep):
    for tower, (feats_ref, emb_ref) in enumerate(
        ((image_ref, image_emb_ref), (text_ref, text_emb_ref))
    ):
        gain = gains_ref[tower : tower + 1, :]
        shift = shifts_ref[tower : tower + 1, :]

        @pl.loop(0, feats_ref.shape[0] // ROW_BLOCK, unroll=UNROLL)
        def _(step):
            rows = pl.ds(pl.multiple_of(step * ROW_BLOCK, ROW_BLOCK), ROW_BLOCK)
            feats = feats_ref[rows, :].astype(jnp.float32)
            _, _, unnormed, inverse = norm_rows(feats, gain, shift)
            emb_ref[rows, :] = (unnormed * inverse).astype(jnp.bfloat16)
            keep[rows, :] = jnp.broadcast_to(inverse, (ROW_BLOCK, 128))

        put_line(emb_ref, to_lanes(keep[:, :1]))


def forward_norms(image_feats, text_feats, gains, shifts):
    rows, width = image_feats.shape
    emb = jax.ShapeDtypeStruct((rows + EXTRA, width), jnp.bfloat16)
    return pl.pallas_call(
        forward_kernel,
        out_shape=(emb, emb),
        scratch_shapes=[pltpu.VMEM((rows, 128), jnp.float32)],
        compiler_params=pltpu.CompilerParams(vmem_limit_bytes=VMEM_LIMIT),
        cost_estimate=pl.CostEstimate(
            flops=40 * rows * width, bytes_accessed=8 * rows * width, transcendentals=0
        ),
        name="forward_norms",
    )(image_feats, text_feats, gains, shifts)


def add_sums(units, parts, inverses):
    along = jnp.sum(units * parts, axis=-1, keepdims=True)
    pulled = parts - units * along
    return (
        jnp.sum(units * pulled, axis=0, keepdims=True),
        jnp.sum(inverses * pulled, axis=0, keepdims=True),
    )


def tile_kernel(final, scalars_ref, gains_ref, shifts_ref, *refs):
    blocks = refs[:4]
    if final:
        image_before, loss_before, sums_before = refs[4:7]
        text_a_ref, text_b_ref, image_ref, back_ref, loss_ref, sums_ref = refs[7:13]
    else:
        text_a_ref, text_b_ref, image_ref, loss_ref, sums_ref = refs[4:9]
    images, texts, coeff = refs[-3:]
    rows = loss_ref.shape[1]
    for at in range(2):
        own = slice(at * rows, (at + 1) * rows)
        images[own, :] = blocks[at][:rows, :]
        texts[own, :] = blocks[2 + at][:rows, :]
    losses = []
    for at in range(2):
        own = slice(at * rows, (at + 1) * rows)
        logits = lax.dot_general(
            images[own, :], texts[...], NT, preferred_element_type=jnp.float32
        )
        logits = scalars_ref[0] * logits + scalars_ref[1]
        diagonal = at == 0 and not final
        if diagonal:
            row_at = lax.broadcasted_iota(jnp.int32, logits.shape, 0)
            column_at = lax.broadcasted_iota(jnp.int32, logits.shape, 1)
            signs = jnp.where(row_at == column_at, -1.0, 1.0)
            logits = signs * logits
        small = jnp.exp(-jnp.abs(logits))
        terms = jnp.maximum(logits, 0.0) + jnp.log1p(small)
        slopes = jnp.where(logits >= 0.0, 1.0, small) / (1.0 + small)
        if diagonal:
            slopes = signs * slopes
        coeff[own, :] = slopes.astype(jnp.bfloat16)
        losses.append(to_lanes(jnp.sum(terms, axis=1, keepdims=True)))
    if final:
        loss_ref[...] = loss_before[:1, :] + losses[0]
        put_line(back_ref, loss_before[1:2, :] + losses[1])
    else:
        for at in range(2):
            loss_ref[at : at + 1, :] = losses[at]

    def inverses(at):
        return to_rows(get_line(blocks[at][rows:, :], rows))

    def finish(tower, unit_sum, shift_sum):
        gain = gains_ref[tower : tower + 1, :]
        shift = shifts_ref[tower : tower + 1, :]
        sums_ref[tower : tower + 1, :] = scalars_ref[0] * (unit_sum - shift * shift_sum) / gain
        sums_ref[2 + tower : 3 + tower, :] = scalars_ref[0] * shift_sum

    unit_sum, shift_sum = 0.0, 0.0
    if final:
        unit_sum, shift_sum = sums_before[:1, :], sums_before[1:2, :]
    for at, part_ref in ((1, text_b_ref), (0, text_a_ref)):
        own = slice(at * rows, (at + 1) * rows)
        part = lax.dot_general(
            coeff[:, own], images[...], TN, preferred_element_type=jnp.float32
        )
        part_ref[...] = part.astype(part_ref.dtype)
        unit_add, shift_add = add_sums(texts[own, :].astype(jnp.float32), part, inverses(2 + at))
        unit_sum, shift_sum = unit_sum + unit_add, shift_sum + shift_add
    if not final:
        sums_ref[:1, :] = unit_sum
        sums_ref[1:2, :] = shift_sum
        image_ref[...] = jnp.dot(coeff[...], texts[...], preferred_element_type=jnp.float32)
        return
    finish(1, unit_sum, shift_sum)
    unit_sum, shift_sum = 0.0, 0.0
    for at in range(2):
        own = slice(at * rows, (at + 1) * rows)
        part = image_before[own, :] + jnp.dot(
            coeff[own, :], texts[...], preferred_element_type=jnp.float32
        )
        if at == 0:
            image_ref[...] = part
        else:
            back_ref[:rows, :] = part.astype(jnp.bfloat16)
        unit_add, shift_add = add_sums(images[own, :].astype(jnp.float32), part, inverses(at))
        unit_sum, shift_sum = unit_sum + unit_add, shift_sum + shift_add
    finish(0, unit_sum, shift_sum)


def tile(scalars, gains, shifts, images, texts, before=()):
    rows, width = images[0].shape[0] - EXTRA, images[0].shape[1]
    final = len(before) > 0
    whole = pl.BlockSpec(memory_space=pltpu.VMEM)

    def wide(count, kind):
        return jax.ShapeDtypeStruct((count, width), kind)

    if final:
        outs = [wide(rows, jnp.bfloat16)] * 2
        outs += [wide(rows, jnp.float32), wide(rows + EXTRA, jnp.bfloat16)]
        outs += [jax.ShapeDtypeStruct((1, rows), jnp.float32), wide(4, jnp.float32)]
    else:
        outs = [wide(rows, jnp.float32)] * 2 + [wide(2 * rows, jnp.float32)]
        outs += [jax.ShapeDtypeStruct((2, rows), jnp.float32), wide(2, jnp.float32)]
    return pl.pallas_call(
        functools.partial(tile_kernel, final),
        out_shape=tuple(outs),
        in_specs=[pl.BlockSpec(memory_space=pltpu.SMEM)] + [whole] * (6 + len(before)),
        out_specs=(whole,) * len(outs),
        scratch_shapes=[
            pltpu.VMEM((2 * rows, width), jnp.bfloat16),
            pltpu.VMEM((2 * rows, width), jnp.bfloat16),
            pltpu.VMEM((2 * rows, 2 * rows), jnp.bfloat16),
        ],
        compiler_params=pltpu.CompilerParams(vmem_limit_bytes=TILE_VMEM_LIMIT),
        cost_estimate=pl.CostEstimate(
            flops=24 * rows * rows * width,
            bytes_accessed=24 * rows * width,
            transcendentals=12 * rows * rows,
        ),
        name="last_tile" if final else "first_tile",
    )(scalars, gains, shifts, *images, *texts, *before)


def backward_kernel(feats_ref, gain_ref, shift_ref, scale_ref, *refs):
    *part_refs, grad_ref = refs

    @pl.loop(0, feats_ref.shape[0] // ROW_BLOCK, unroll=UNROLL)
    def _(step):
        rows = pl.ds(pl.multiple_of(step * ROW_BLOCK, ROW_BLOCK), ROW_BLOCK)
        feats = feats_ref[rows, :].astype(jnp.float32)
        gain = gain_ref[...]
        normed, rstd, unnormed, inverse = norm_rows(feats, gain, shift_ref[...])
        unit = unnormed * inverse
        pulled = part_refs[0][rows, :].astype(jnp.float32)
        for part_ref in part_refs[1:]:
            pulled = pulled + part_ref[rows, :].astype(jnp.float32)
        pulled = pulled * scale_ref[0]
        along = jnp.sum(unit * pulled, axis=-1, keepdims=True)
        pulled = inverse * (pulled - unit * along) * gain
        pulled = pulled - normed * jnp.mean(pulled * normed, axis=-1, keepdims=True)
        pulled = rstd * (pulled - jnp.mean(pulled, axis=-1, keepdims=True))
        grad_ref[rows, :] = pulled.astype(jnp.bfloat16)


def backward_norm(feats, gain, shift, scale, parts):
    rows, width = feats.shape
    whole = pl.BlockSpec(memory_space=pltpu.VMEM)
    return pl.pallas_call(
        backward_kernel,
        out_shape=jax.ShapeDtypeStruct((rows, width), jnp.bfloat16),
        in_specs=[whole] * 3 + [pl.BlockSpec(memory_space=pltpu.SMEM)] + [whole] * len(parts),
        out_specs=whole,
        compiler_params=pltpu.CompilerParams(vmem_limit_bytes=VMEM_LIMIT),
        cost_estimate=pl.CostEstimate(
            flops=40 * rows * width, bytes_accessed=12 * rows * width, transcendentals=0
        ),
        name="backward_norm",
    )(feats, gain, shift, scale, *parts)


def near(place):
    return place ^ 1


def far(place):
    return RING - 1 - place


class Routes:
    def __init__(self, sizes):
        self.sizes = sizes
        y_lo, z_hi, z_lo, x, y_hi, core = sizes
        self.count = y_lo * z_hi * z_lo * x * y_hi * core

    def split(self, index):
        place = []
        for size in reversed(self.sizes):
            place.append(index % size)
            index //= size
        return place[::-1]

    def join(self, place):
        index = 0
        for size, at in zip(self.sizes, place):
            index = index * size + at
        return index

    def pairs(self, move):
        out = []
        for index in range(self.count):
            place = self.split(index)
            out.append((index, self.join(move(list(place)))))
        return out

    def along(self, axis, step):
        def move(place):
            place[axis] = step(place[axis])
            return place

        return self.pairs(move)

    def across_y(self):
        return self.along(0, near)

    def towers(self):
        def text(place):
            place[1] = far(place[1]) if place[5] == 0 else near(place[1])
            return place

        def image(place):
            place[1] = near(place[1]) if place[5] == 0 else far(place[1])
            return place

        return self.pairs(text), self.pairs(image)

    def ring(self, high, low):
        size = self.sizes[low] * (1 if high is None else self.sizes[high])
        steps = []
        reach = -1
        while 2 ** len(steps) < size:

            def move(place, reach=reach):
                at = place[low] + (0 if high is None else place[high] * self.sizes[low])
                at = (at + (reach if at % 2 else -reach)) % size
                place[low] = at % self.sizes[low]
                if high is not None:
                    place[high] = at // self.sizes[low]
                return place

            steps.append(self.pairs(move))
            reach = -2 * reach - 1
        return steps


def send(value, pairs):
    return lax.ppermute(value, AXES, pairs)


def sum_over(value, steps, turns):
    def one(carry):
        turn, value = carry
        for pairs in steps:
            value = value + send(value, pairs)
        return turn + 1, value

    return lax.while_loop(lambda carry: carry[0] < turns, one, (jnp.int32(0), value))[1]


def make_body(routes):
    text_pairs, image_pairs = routes.towers()
    y_pairs = routes.across_y()
    z_steps = routes.ring(1, 2)
    flat_steps = [routes.along(5, near), *routes.ring(None, 3), *routes.ring(4, 0)]
    early_steps, middle_steps = flat_steps[:2], flat_steps[2:]
    group_rows = 2 * RING

    def body(image_feats, text_feats, gains, shifts, log_scale, logit_bias):
        scale = jnp.exp(log_scale)
        scalars = jnp.concatenate([scale, logit_bias])
        turns = jnp.where(log_scale[0] == log_scale[0], 1, 0)
        image, text = forward_norms(image_feats[0], text_feats[0], gains, shifts)
        rows = image_feats.shape[1]

        text_z = send(text, text_pairs)
        image_z = send(image, image_pairs)
        text_y = send(text, y_pairs)
        text_zy = send(text_z, y_pairs)
        images = [image, image_z]
        text_part, text_z_part, *before = tile(scalars, gains, shifts, images, [text, text_z])
        text_y_part, text_zy_part, image_part, image_z_part, loss_own, sums = tile(
            scalars, gains, shifts, images, [text_y, text_zy], before
        )

        text_zy_back = send(text_zy_part, y_pairs)
        image_back = send(image_z_part, image_pairs)
        sums = sum_over(sums, early_steps, turns)
        sums, text_zy_back, text_y_part = lax.optimization_barrier(
            (sums, text_zy_back, text_y_part)
        )
        text_z_sum = text_z_part + text_zy_back.astype(jnp.float32)
        text_z_back = send(text_z_sum.astype(jnp.bfloat16), text_pairs)
        text_y_back = send(text_y_part, y_pairs)
        sums = sum_over(sums, middle_steps, turns)
        sums, image_back = lax.optimization_barrier((sums, image_back))
        image_grad = backward_norm(
            image_feats[0], gains[:1], shifts[:1], scale, [image_part, image_back]
        )
        for pairs in z_steps:
            sums = sums + send(sums, pairs)
        text_grad = backward_norm(
            text_feats[0],
            gains[1:],
            shifts[1:],
            scale,
            [text_part, text_y_back, text_z_back],
        )

        row_mean = (loss_own + get_line(image_back[rows:], rows)) / (group_rows * rows)
        return (image_grad[None], text_grad[None], sums[:2], sums[2:], row_mean)

    return body


def build(mesh, sizes):
    placed = (P("dp", "img", None), P("dp", "img", None), P(), P(), P(), P())
    return jax.shard_map(
        make_body(Routes(sizes)),
        mesh=mesh,
        in_specs=placed,
        out_specs=(P("dp", "img", None), P("dp", "img", None), P(), P(), P("dp", "img")),
        check_vma=False,
    )


def solution(mesh):
    y_high, cores = Y_HIGH, mesh.shape["dp"] // Y_HIGH
    y_low = mesh.shape["img"] // (RING * Z_BLOCK * X_CHIPS)
    return build(mesh, (y_low, RING, Z_BLOCK, X_CHIPS, y_high, cores))
```

```python
import functools

import jax
import jax.numpy as jnp
from jax import lax
from jax.experimental import pallas as pl
from jax.experimental.pallas import tpu as pltpu
from jax.sharding import PartitionSpec as P

AXES = ("img", "dp")
RING = 4
X_CHIPS = 4
Z_BLOCK = 4
Y_HIGH = 4

VMEM_LIMIT = 60 << 20
TILE_VMEM_LIMIT = 24 << 20
ROW_BLOCK = 16
UNROLL = 4
EPS = 1e-06
EXTRA = 16
LANES = 256
NT = (((1,), (1,)), ((), ()))
TN = (((0,), (0,)), ((), ()))


def to_lanes(column):
    count = column.shape[0]
    on = lax.broadcasted_iota(jnp.int32, (count, count), 0) == lax.broadcasted_iota(
        jnp.int32, (count, count), 1
    )
    return jnp.sum(jnp.where(on, column, 0.0), axis=0, keepdims=True)


def to_rows(line):
    count = line.shape[1]
    on = lax.broadcasted_iota(jnp.int32, (count, count), 0) == lax.broadcasted_iota(
        jnp.int32, (count, count), 1
    )
    return jnp.sum(jnp.where(on, line, 0.0), axis=1, keepdims=True)


def put_line(ref, line):
    count = line.shape[1]
    rows = ref.shape[0] - EXTRA
    ref[rows:, :] = jnp.zeros((EXTRA, ref.shape[1]), ref.dtype)
    for term in range(3):
        piece = line.astype(jnp.bfloat16)
        line = line - piece.astype(jnp.float32)
        ref[rows:, term * LANES : term * LANES + count] = jnp.broadcast_to(piece, (EXTRA, count))


def get_line(block, count):
    terms = [
        block[:1, term * LANES : term * LANES + count].astype(jnp.float32) for term in range(3)
    ]
    return terms[0] + (terms[1] + terms[2])


def norm_rows(feats, gain, shift):
    center = jnp.mean(feats, axis=-1, keepdims=True)
    offset = feats - center
    spread = jnp.mean(offset * offset, axis=-1, keepdims=True)
    rstd = lax.rsqrt(spread + EPS)
    normed = offset * rstd
    unnormed = normed * gain + shift
    inverse = lax.rsqrt(jnp.sum(unnormed * unnormed, axis=-1, keepdims=True) + EPS)
    return normed, rstd, unnormed, inverse


def forward_kernel(image_ref, text_ref, gains_ref, shifts_ref, image_emb_ref, text_emb_ref, keep):
    for tower, (feats_ref, emb_ref) in enumerate(
        ((image_ref, image_emb_ref), (text_ref, text_emb_ref))
    ):
        gain = gains_ref[tower : tower + 1, :]
        shift = shifts_ref[tower : tower + 1, :]

        @pl.loop(0, feats_ref.shape[0] // ROW_BLOCK, unroll=UNROLL)
        def _(step):
            rows = pl.ds(pl.multiple_of(step * ROW_BLOCK, ROW_BLOCK), ROW_BLOCK)
            feats = feats_ref[rows, :].astype(jnp.float32)
            _, _, unnormed, inverse = norm_rows(feats, gain, shift)
            emb_ref[rows, :] = (unnormed * inverse).astype(jnp.bfloat16)
            keep[rows, :] = jnp.broadcast_to(inverse, (ROW_BLOCK, 128))

        put_line(emb_ref, to_lanes(keep[:, :1]))


def forward_norms(image_feats, text_feats, gains, shifts):
    rows, width = image_feats.shape
    emb = jax.ShapeDtypeStruct((rows + EXTRA, width), jnp.bfloat16)
    return pl.pallas_call(
        forward_kernel,
        out_shape=(emb, emb),
        scratch_shapes=[pltpu.VMEM((rows, 128), jnp.float32)],
        compiler_params=pltpu.CompilerParams(vmem_limit_bytes=VMEM_LIMIT),
        cost_estimate=pl.CostEstimate(
            flops=40 * rows * width, bytes_accessed=8 * rows * width, transcendentals=0
        ),
        name="forward_norms",
    )(image_feats, text_feats, gains, shifts)


def add_sums(units, parts, inverses):
    along = jnp.sum(units * parts, axis=-1, keepdims=True)
    pulled = parts - units * along
    return (
        jnp.sum(units * pulled, axis=0, keepdims=True),
        jnp.sum(inverses * pulled, axis=0, keepdims=True),
    )


def tile_kernel(final, scalars_ref, gains_ref, shifts_ref, *refs):
    blocks = refs[:4]
    if final:
        image_before, loss_before, sums_before = refs[4:7]
        texts_ref, image_ref, back_ref, loss_ref, sums_ref = refs[7:12]
    else:
        text_a_ref, text_b_ref, image_ref, loss_ref, sums_ref = refs[4:9]
        texts_ref = None
    images, texts, coeff = refs[-3:]
    rows = loss_ref.shape[1]
    for at in range(2):
        own = slice(at * rows, (at + 1) * rows)
        images[own, :] = blocks[at][:rows, :]
        texts[own, :] = blocks[2 + at][:rows, :]
    losses = []
    for at in range(2):
        own = slice(at * rows, (at + 1) * rows)
        logits = lax.dot_general(
            images[own, :], texts[...], NT, preferred_element_type=jnp.float32
        )
        logits = scalars_ref[0] * logits + scalars_ref[1]
        diagonal = at == 0 and not final
        if diagonal:
            row_at = lax.broadcasted_iota(jnp.int32, logits.shape, 0)
            column_at = lax.broadcasted_iota(jnp.int32, logits.shape, 1)
            signs = jnp.where(row_at == column_at, -1.0, 1.0)
            logits = signs * logits
        small = jnp.exp(-jnp.abs(logits))
        terms = jnp.maximum(logits, 0.0) + jnp.log1p(small)
        slopes = jnp.where(logits >= 0.0, 1.0, small) / (1.0 + small)
        if diagonal:
            slopes = signs * slopes
        coeff[own, :] = slopes.astype(jnp.bfloat16)
        losses.append(to_lanes(jnp.sum(terms, axis=1, keepdims=True)))
    if final:
        loss_ref[...] = loss_before[:1, :] + losses[0]
        put_line(back_ref, loss_before[1:2, :] + losses[1])
    else:
        for at in range(2):
            loss_ref[at : at + 1, :] = losses[at]

    def inverses(at):
        return to_rows(get_line(blocks[at][rows:, :], rows))

    def finish(tower, unit_sum, shift_sum):
        gain = gains_ref[tower : tower + 1, :]
        shift = shifts_ref[tower : tower + 1, :]
        sums_ref[tower : tower + 1, :] = scalars_ref[0] * (unit_sum - shift * shift_sum) / gain
        sums_ref[2 + tower : 3 + tower, :] = scalars_ref[0] * shift_sum

    unit_sum, shift_sum = 0.0, 0.0
    if final:
        unit_sum, shift_sum = sums_before[:1, :], sums_before[1:2, :]
    for at in (1, 0):
        own = slice(at * rows, (at + 1) * rows)
        part = lax.dot_general(
            coeff[:, own], images[...], TN, preferred_element_type=jnp.float32
        )
        if final:
            texts_ref[(1 - at) * rows : (2 - at) * rows, :] = part.astype(jnp.bfloat16)
        else:
            (text_a_ref, text_b_ref)[at][...] = part
        unit_add, shift_add = add_sums(texts[own, :].astype(jnp.float32), part, inverses(2 + at))
        unit_sum, shift_sum = unit_sum + unit_add, shift_sum + shift_add
    if not final:
        sums_ref[:1, :] = unit_sum
        sums_ref[1:2, :] = shift_sum
        image_ref[...] = jnp.dot(coeff[...], texts[...], preferred_element_type=jnp.float32)
        return
    finish(1, unit_sum, shift_sum)
    unit_sum, shift_sum = 0.0, 0.0
    for at in range(2):
        own = slice(at * rows, (at + 1) * rows)
        part = image_before[own, :] + jnp.dot(
            coeff[own, :], texts[...], preferred_element_type=jnp.float32
        )
        if at == 0:
            image_ref[...] = part
        else:
            back_ref[:rows, :] = part.astype(jnp.bfloat16)
        unit_add, shift_add = add_sums(images[own, :].astype(jnp.float32), part, inverses(at))
        unit_sum, shift_sum = unit_sum + unit_add, shift_sum + shift_add
    finish(0, unit_sum, shift_sum)


def tile(scalars, gains, shifts, images, texts, before=()):
    rows, width = images[0].shape[0] - EXTRA, images[0].shape[1]
    final = len(before) > 0
    whole = pl.BlockSpec(memory_space=pltpu.VMEM)

    def wide(count, kind):
        return jax.ShapeDtypeStruct((count, width), kind)

    if final:
        outs = [wide(2 * rows, jnp.bfloat16)]
        outs += [wide(rows, jnp.float32), wide(rows + EXTRA, jnp.bfloat16)]
        outs += [jax.ShapeDtypeStruct((1, rows), jnp.float32), wide(4, jnp.float32)]
    else:
        outs = [wide(rows, jnp.float32)] * 2 + [wide(2 * rows, jnp.float32)]
        outs += [jax.ShapeDtypeStruct((2, rows), jnp.float32), wide(2, jnp.float32)]
    return pl.pallas_call(
        functools.partial(tile_kernel, final),
        out_shape=tuple(outs),
        in_specs=[pl.BlockSpec(memory_space=pltpu.SMEM)] + [whole] * (6 + len(before)),
        out_specs=(whole,) * len(outs),
        scratch_shapes=[
            pltpu.VMEM((2 * rows, width), jnp.bfloat16),
            pltpu.VMEM((2 * rows, width), jnp.bfloat16),
            pltpu.VMEM((2 * rows, 2 * rows), jnp.bfloat16),
        ],
        compiler_params=pltpu.CompilerParams(vmem_limit_bytes=TILE_VMEM_LIMIT),
        cost_estimate=pl.CostEstimate(
            flops=24 * rows * rows * width,
            bytes_accessed=24 * rows * width,
            transcendentals=12 * rows * rows,
        ),
        name="last_tile" if final else "first_tile",
    )(scalars, gains, shifts, *images, *texts, *before)


def backward_kernel(firsts, feats_ref, gain_ref, shift_ref, scale_ref, *refs):
    *part_refs, grad_ref = refs

    @pl.loop(0, feats_ref.shape[0] // ROW_BLOCK, unroll=UNROLL)
    def _(step):
        rows = pl.ds(pl.multiple_of(step * ROW_BLOCK, ROW_BLOCK), ROW_BLOCK)
        feats = feats_ref[rows, :].astype(jnp.float32)
        gain = gain_ref[...]
        normed, rstd, unnormed, inverse = norm_rows(feats, gain, shift_ref[...])
        unit = unnormed * inverse
        pulled = 0.0
        for first, part_ref in zip(firsts, part_refs):
            at = pl.ds(pl.multiple_of(first + step * ROW_BLOCK, ROW_BLOCK), ROW_BLOCK)
            pulled = pulled + part_ref[at, :].astype(jnp.float32)
        pulled = pulled * scale_ref[0]
        along = jnp.sum(unit * pulled, axis=-1, keepdims=True)
        pulled = inverse * (pulled - unit * along) * gain
        pulled = pulled - normed * jnp.mean(pulled * normed, axis=-1, keepdims=True)
        pulled = rstd * (pulled - jnp.mean(pulled, axis=-1, keepdims=True))
        grad_ref[rows, :] = pulled.astype(jnp.bfloat16)


def backward_norm(feats, gain, shift, scale, parts):
    rows, width = feats.shape
    firsts = [first for first, _ in parts]
    parts = [part for _, part in parts]
    whole = pl.BlockSpec(memory_space=pltpu.VMEM)
    return pl.pallas_call(
        functools.partial(backward_kernel, firsts),
        out_shape=jax.ShapeDtypeStruct((rows, width), jnp.bfloat16),
        in_specs=[whole] * 3 + [pl.BlockSpec(memory_space=pltpu.SMEM)] + [whole] * len(parts),
        out_specs=whole,
        compiler_params=pltpu.CompilerParams(vmem_limit_bytes=VMEM_LIMIT),
        cost_estimate=pl.CostEstimate(
            flops=40 * rows * width, bytes_accessed=12 * rows * width, transcendentals=0
        ),
        name="backward_norm",
    )(feats, gain, shift, scale, *parts)


def near(place):
    return place ^ 1


def far(place):
    return RING - 1 - place


class Routes:
    def __init__(self, sizes):
        self.sizes = sizes
        y_lo, z_hi, z_lo, x, y_hi, core = sizes
        self.count = y_lo * z_hi * z_lo * x * y_hi * core

    def split(self, index):
        place = []
        for size in reversed(self.sizes):
            place.append(index % size)
            index //= size
        return place[::-1]

    def join(self, place):
        index = 0
        for size, at in zip(self.sizes, place):
            index = index * size + at
        return index

    def pairs(self, move):
        out = []
        for index in range(self.count):
            place = self.split(index)
            out.append((index, self.join(move(list(place)))))
        return out

    def along(self, axis, step):
        def move(place):
            place[axis] = step(place[axis])
            return place

        return self.pairs(move)

    def across_y(self):
        return self.along(0, near)

    def towers(self):
        def text(place):
            place[1] = far(place[1]) if place[5] == 0 else near(place[1])
            return place

        def image(place):
            place[1] = near(place[1]) if place[5] == 0 else far(place[1])
            return place

        return self.pairs(text), self.pairs(image)

    def ring(self, high, low):
        size = self.sizes[low] * (1 if high is None else self.sizes[high])
        steps = []
        reach = -1
        while 2 ** len(steps) < size:

            def move(place, reach=reach):
                at = place[low] + (0 if high is None else place[high] * self.sizes[low])
                at = (at + (reach if at % 2 else -reach)) % size
                place[low] = at % self.sizes[low]
                if high is not None:
                    place[high] = at // self.sizes[low]
                return place

            steps.append(self.pairs(move))
            reach = -2 * reach - 1
        return steps


def send(value, pairs):
    return lax.ppermute(value, AXES, pairs)


def sum_over(value, steps, turns):
    def one(carry):
        turn, value = carry
        for pairs in steps:
            value = value + send(value, pairs)
        return turn + 1, value

    return lax.while_loop(lambda carry: carry[0] < turns, one, (jnp.int32(0), value))[1]


def make_body(routes):
    text_pairs, image_pairs = routes.towers()
    y_pairs = routes.across_y()
    z_steps = routes.ring(1, 2)
    flat_steps = [routes.along(5, near), *routes.ring(None, 3), *routes.ring(4, 0)]
    early_steps, middle_steps = flat_steps[:3], flat_steps[3:] + z_steps[:-2]
    late_steps = z_steps[-2:]
    group_rows = 2 * RING

    def body(image_feats, text_feats, gains, shifts, log_scale, logit_bias):
        scale = jnp.exp(log_scale)
        scalars = jnp.concatenate([scale, logit_bias])
        turns = jnp.where(log_scale[0] == log_scale[0], 1, 0)
        image, text = forward_norms(image_feats[0], text_feats[0], gains, shifts)
        rows = image_feats.shape[1]

        text_z = send(text, text_pairs)
        image_z = send(image, image_pairs)
        text_y = send(text, y_pairs)
        text_zy = send(text_z, y_pairs)
        images = [image, image_z]
        text_part, text_z_part, *before = tile(scalars, gains, shifts, images, [text, text_z])
        y_parts, image_part, image_z_part, loss_own, sums = tile(
            scalars, gains, shifts, images, [text_y, text_zy], before
        )

        image_back = send(image_z_part, image_pairs)
        y_back = send(y_parts, y_pairs)
        sums = sum_over(sums, early_steps, turns)
        sums, y_back = lax.optimization_barrier((sums, y_back))
        text_z_sum = text_z_part + y_back[:rows].astype(jnp.float32)
        text_z_back = send(text_z_sum.astype(jnp.bfloat16), text_pairs)
        sums = sum_over(sums, middle_steps, turns)
        sums, image_back, text_z_back = lax.optimization_barrier((sums, image_back, text_z_back))
        image_grad = backward_norm(
            image_feats[0], gains[:1], shifts[:1], scale, [(0, image_part), (0, image_back)]
        )
        sums = sums + send(sums, late_steps[0])
        sums, image_grad = lax.optimization_barrier((sums, image_grad))
        for pairs in late_steps[1:]:
            sums = sums + send(sums, pairs)
        text_grad = backward_norm(
            text_feats[0],
            gains[1:],
            shifts[1:],
            scale,
            [(0, text_part), (rows, y_back), (0, text_z_back)],
        )

        row_mean = (loss_own + get_line(image_back[rows:], rows)) / (group_rows * rows)
        return (image_grad[None], text_grad[None], sums[:2], sums[2:], row_mean)

    return body


def build(mesh, sizes):
    placed = (P("dp", "img", None), P("dp", "img", None), P(), P(), P(), P())
    return jax.shard_map(
        make_body(Routes(sizes)),
        mesh=mesh,
        in_specs=placed,
        out_specs=(P("dp", "img", None), P("dp", "img", None), P(), P(), P("dp", "img")),
        check_vma=False,
    )


def solution(mesh):
    y_high, cores = Y_HIGH, mesh.shape["dp"] // Y_HIGH
    y_low = mesh.shape["img"] // (RING * Z_BLOCK * X_CHIPS)
    return build(mesh, (y_low, RING, Z_BLOCK, X_CHIPS, y_high, cores))
```

```python
import functools

import jax
import jax.numpy as jnp
from jax import lax
from jax.experimental import pallas as pl
from jax.experimental.pallas import tpu as pltpu
from jax.sharding import PartitionSpec as P

AXES = ("img", "dp")
RING = 4
X_CHIPS = 4
Z_BLOCK = 4
Y_HIGH = 4

VMEM_LIMIT = 60 << 20
TILE_VMEM_LIMIT = 24 << 20
ROW_BLOCK = 16
UNROLL = 4
EPS = 1e-06
EXTRA = 16
LANES = 256
NT = (((1,), (1,)), ((), ()))
TN = (((0,), (0,)), ((), ()))


def to_lanes(column):
    count = column.shape[0]
    on = lax.broadcasted_iota(jnp.int32, (count, count), 0) == lax.broadcasted_iota(
        jnp.int32, (count, count), 1
    )
    return jnp.sum(jnp.where(on, column, 0.0), axis=0, keepdims=True)


def to_rows(line):
    count = line.shape[1]
    on = lax.broadcasted_iota(jnp.int32, (count, count), 0) == lax.broadcasted_iota(
        jnp.int32, (count, count), 1
    )
    return jnp.sum(jnp.where(on, line, 0.0), axis=1, keepdims=True)


def put_line(ref, line):
    count = line.shape[1]
    rows = ref.shape[0] - EXTRA
    ref[rows:, :] = jnp.zeros((EXTRA, ref.shape[1]), ref.dtype)
    for term in range(3):
        piece = line.astype(jnp.bfloat16)
        line = line - piece.astype(jnp.float32)
        ref[rows:, term * LANES : term * LANES + count] = jnp.broadcast_to(piece, (EXTRA, count))


def get_line(block, count):
    terms = [
        block[:1, term * LANES : term * LANES + count].astype(jnp.float32) for term in range(3)
    ]
    return terms[0] + (terms[1] + terms[2])


def norm_rows(feats, gain, shift):
    center = jnp.mean(feats, axis=-1, keepdims=True)
    offset = feats - center
    spread = jnp.mean(offset * offset, axis=-1, keepdims=True)
    rstd = lax.rsqrt(spread + EPS)
    normed = offset * rstd
    unnormed = normed * gain + shift
    inverse = lax.rsqrt(jnp.sum(unnormed * unnormed, axis=-1, keepdims=True) + EPS)
    return normed, rstd, unnormed, inverse


def forward_kernel(image_ref, text_ref, gains_ref, shifts_ref, image_emb_ref, text_emb_ref, keep):
    for tower, (feats_ref, emb_ref) in enumerate(
        ((image_ref, image_emb_ref), (text_ref, text_emb_ref))
    ):
        gain = gains_ref[tower : tower + 1, :]
        shift = shifts_ref[tower : tower + 1, :]

        @pl.loop(0, feats_ref.shape[0] // ROW_BLOCK, unroll=UNROLL)
        def _(step):
            rows = pl.ds(pl.multiple_of(step * ROW_BLOCK, ROW_BLOCK), ROW_BLOCK)
            feats = feats_ref[rows, :].astype(jnp.float32)
            _, _, unnormed, inverse = norm_rows(feats, gain, shift)
            emb_ref[rows, :] = (unnormed * inverse).astype(jnp.bfloat16)
            keep[rows, :] = jnp.broadcast_to(inverse, (ROW_BLOCK, 128))

        put_line(emb_ref, to_lanes(keep[:, :1]))


def forward_norms(image_feats, text_feats, gains, shifts):
    rows, width = image_feats.shape
    emb = jax.ShapeDtypeStruct((rows + EXTRA, width), jnp.bfloat16)
    return pl.pallas_call(
        forward_kernel,
        out_shape=(emb, emb),
        scratch_shapes=[pltpu.VMEM((rows, 128), jnp.float32)],
        compiler_params=pltpu.CompilerParams(vmem_limit_bytes=VMEM_LIMIT),
        cost_estimate=pl.CostEstimate(
            flops=40 * rows * width, bytes_accessed=8 * rows * width, transcendentals=0
        ),
        name="forward_norms",
    )(image_feats, text_feats, gains, shifts)


def add_sums(units, parts, inverses):
    along = jnp.sum(units * parts, axis=-1, keepdims=True)
    pulled = parts - units * along
    return (
        jnp.sum(units * pulled, axis=0, keepdims=True),
        jnp.sum(inverses * pulled, axis=0, keepdims=True),
    )


def tile_kernel(final, scalars_ref, gains_ref, shifts_ref, *refs):
    image_in, text_ins = refs[0], refs[1:5]
    if final:
        parts_before, sums_before = refs[5:7]
        text_ref, text_z_ref, texts_ref, image_ref, sums_ref = refs[7:12]
    else:
        parts_ref, image_ref, loss_ref, sums_ref = refs[5:9]
    texts, coeff = refs[-2:]
    rows = coeff.shape[0]
    image = image_in[:rows, :]
    for at, ref in enumerate(text_ins):
        texts[at * rows : (at + 1) * rows, :] = ref[:rows, :]
    logits = lax.dot_general(image, texts[...], NT, preferred_element_type=jnp.float32)
    logits = scalars_ref[0] * logits + scalars_ref[1]
    if not final:
        row_at = lax.broadcasted_iota(jnp.int32, logits.shape, 0)
        column_at = lax.broadcasted_iota(jnp.int32, logits.shape, 1)
        signs = jnp.where(row_at == column_at, -1.0, 1.0)
        logits = signs * logits
    small = jnp.exp(-jnp.abs(logits))
    terms = jnp.maximum(logits, 0.0) + jnp.log1p(small)
    slopes = jnp.where(logits >= 0.0, 1.0, small) / (1.0 + small)
    if not final:
        slopes = signs * slopes
    coeff[...] = slopes.astype(jnp.bfloat16)
    losses = to_lanes(jnp.sum(terms, axis=1, keepdims=True))
    if final:
        put_line(image_ref, losses)
    else:
        loss_ref[...] = losses

    unit_sum, shift_sum = 0.0, 0.0
    for at in (3, 2, 1, 0):
        own = slice(at * rows, (at + 1) * rows)
        part = lax.dot_general(coeff[:, own], image, TN, preferred_element_type=jnp.float32)
        if not final:
            parts_ref[own, :] = part
        elif at >= 2:
            whole = part + parts_before[own, :]
            texts_ref[(3 - at) * rows : (4 - at) * rows, :] = whole.astype(jnp.bfloat16)
        else:
            (text_ref, text_z_ref)[at][...] = part + parts_before[own, :]
        inverse = to_rows(get_line(text_ins[at][rows:, :], rows))
        unit_add, shift_add = add_sums(texts[own, :].astype(jnp.float32), part, inverse)
        unit_sum, shift_sum = unit_sum + unit_add, shift_sum + shift_add
    part = jnp.dot(coeff[...], texts[...], preferred_element_type=jnp.float32)
    if final:
        image_ref[:rows, :] = part.astype(jnp.bfloat16)
    else:
        image_ref[...] = part
    inverse = to_rows(get_line(image_in[rows:, :], rows))
    image_unit_sum, image_shift_sum = add_sums(image.astype(jnp.float32), part, inverse)
    sums = (image_unit_sum, unit_sum, image_shift_sum, shift_sum)
    if not final:
        for at in range(4):
            sums_ref[at : at + 1, :] = sums[at]
        return
    for tower in range(2):
        shift = shifts_ref[tower : tower + 1, :]
        unit_sum = sums[tower] + sums_before[tower : tower + 1, :]
        shift_sum = sums[2 + tower] + sums_before[2 + tower : 3 + tower, :]
        gain_sum = (unit_sum - shift * shift_sum) / gains_ref[tower : tower + 1, :]
        sums_ref[tower : tower + 1, :] = scalars_ref[0] * gain_sum
        sums_ref[2 + tower : 3 + tower, :] = scalars_ref[0] * shift_sum


def tile(scalars, gains, shifts, image, texts, before=()):
    rows, width = image.shape[0] - EXTRA, image.shape[1]
    final = len(before) > 0
    whole = pl.BlockSpec(memory_space=pltpu.VMEM)

    def wide(count, kind):
        return jax.ShapeDtypeStruct((count, width), kind)

    if final:
        outs = [wide(rows, jnp.float32)] * 2
        outs += [wide(2 * rows, jnp.bfloat16), wide(rows + EXTRA, jnp.bfloat16)]
    else:
        outs = [wide(4 * rows, jnp.float32), wide(rows, jnp.float32)]
        outs += [jax.ShapeDtypeStruct((1, rows), jnp.float32)]
    outs += [wide(4, jnp.float32)]
    return pl.pallas_call(
        functools.partial(tile_kernel, final),
        out_shape=tuple(outs),
        in_specs=[pl.BlockSpec(memory_space=pltpu.SMEM)] + [whole] * (7 + len(before)),
        out_specs=(whole,) * len(outs),
        scratch_shapes=[
            pltpu.VMEM((4 * rows, width), jnp.bfloat16),
            pltpu.VMEM((rows, 4 * rows), jnp.bfloat16),
        ],
        compiler_params=pltpu.CompilerParams(vmem_limit_bytes=TILE_VMEM_LIMIT),
        cost_estimate=pl.CostEstimate(
            flops=24 * rows * rows * width,
            bytes_accessed=24 * rows * width,
            transcendentals=12 * rows * rows,
        ),
        name="last_tile" if final else "first_tile",
    )(scalars, gains, shifts, image, *texts, *before)


def backward_kernel(firsts, feats_ref, gain_ref, shift_ref, scale_ref, *refs):
    *part_refs, grad_ref = refs

    @pl.loop(0, feats_ref.shape[0] // ROW_BLOCK, unroll=UNROLL)
    def _(step):
        rows = pl.ds(pl.multiple_of(step * ROW_BLOCK, ROW_BLOCK), ROW_BLOCK)
        feats = feats_ref[rows, :].astype(jnp.float32)
        gain = gain_ref[...]
        normed, rstd, unnormed, inverse = norm_rows(feats, gain, shift_ref[...])
        unit = unnormed * inverse
        pulled = 0.0
        for first, part_ref in zip(firsts, part_refs):
            at = pl.ds(pl.multiple_of(first + step * ROW_BLOCK, ROW_BLOCK), ROW_BLOCK)
            pulled = pulled + part_ref[at, :].astype(jnp.float32)
        pulled = pulled * scale_ref[0]
        along = jnp.sum(unit * pulled, axis=-1, keepdims=True)
        pulled = inverse * (pulled - unit * along) * gain
        pulled = pulled - normed * jnp.mean(pulled * normed, axis=-1, keepdims=True)
        pulled = rstd * (pulled - jnp.mean(pulled, axis=-1, keepdims=True))
        grad_ref[rows, :] = pulled.astype(jnp.bfloat16)


def backward_norm(feats, gain, shift, scale, parts):
    rows, width = feats.shape
    firsts = [first for first, _ in parts]
    parts = [part for _, part in parts]
    whole = pl.BlockSpec(memory_space=pltpu.VMEM)
    return pl.pallas_call(
        functools.partial(backward_kernel, firsts),
        out_shape=jax.ShapeDtypeStruct((rows, width), jnp.bfloat16),
        in_specs=[whole] * 3 + [pl.BlockSpec(memory_space=pltpu.SMEM)] + [whole] * len(parts),
        out_specs=whole,
        compiler_params=pltpu.CompilerParams(vmem_limit_bytes=VMEM_LIMIT),
        cost_estimate=pl.CostEstimate(
            flops=40 * rows * width, bytes_accessed=12 * rows * width, transcendentals=0
        ),
        name="backward_norm",
    )(feats, gain, shift, scale, *parts)


def near(place):
    return place ^ 1


def far(place):
    return RING - 1 - place


class Routes:
    def __init__(self, sizes):
        self.sizes = sizes
        y_lo, z_hi, z_lo, x, y_hi, core = sizes
        self.count = y_lo * z_hi * z_lo * x * y_hi * core

    def split(self, index):
        place = []
        for size in reversed(self.sizes):
            place.append(index % size)
            index //= size
        return place[::-1]

    def join(self, place):
        index = 0
        for size, at in zip(self.sizes, place):
            index = index * size + at
        return index

    def pairs(self, move):
        out = []
        for index in range(self.count):
            place = self.split(index)
            out.append((index, self.join(move(list(place)))))
        return out

    def along(self, axis, step):
        def move(place):
            place[axis] = step(place[axis])
            return place

        return self.pairs(move)

    def across_y(self):
        return self.along(0, near)

    def towers(self):
        def text(place):
            place[1] = far(place[1]) if place[5] == 0 else near(place[1])
            return place

        def image(place):
            place[1] = near(place[1]) if place[5] == 0 else far(place[1])
            return place

        return self.pairs(text), self.pairs(image)

    def ring(self, high, low):
        size = self.sizes[low] * (1 if high is None else self.sizes[high])
        steps = []
        reach = -1
        while 2 ** len(steps) < size:

            def move(place, reach=reach):
                at = place[low] + (0 if high is None else place[high] * self.sizes[low])
                at = (at + (reach if at % 2 else -reach)) % size
                place[low] = at % self.sizes[low]
                if high is not None:
                    place[high] = at // self.sizes[low]
                return place

            steps.append(self.pairs(move))
            reach = -2 * reach - 1
        return steps


def send(value, pairs):
    return lax.ppermute(value, AXES, pairs)


def sum_over(value, steps, turns):
    def one(carry):
        turn, value = carry
        for pairs in steps:
            value = value + send(value, pairs)
        return turn + 1, value

    return lax.while_loop(lambda carry: carry[0] < turns, one, (jnp.int32(0), value))[1]


def make_body(routes):
    text_pairs, image_pairs = routes.towers()
    y_pairs = routes.across_y()
    z_steps = routes.ring(1, 2)
    flat_steps = [routes.along(5, near), *routes.ring(None, 3), *routes.ring(4, 0)]
    early_steps, middle_steps = flat_steps[:4], flat_steps[4:] + z_steps[:-2]
    late_steps = z_steps[-2:]
    group_rows = 2 * RING

    def body(image_feats, text_feats, gains, shifts, log_scale, logit_bias):
        scale = jnp.exp(log_scale)
        scalars = jnp.concatenate([scale, logit_bias])
        turns = jnp.where(log_scale[0] == log_scale[0], 1, 0)
        image, text = forward_norms(image_feats[0], text_feats[0], gains, shifts)
        rows = image_feats.shape[1]

        text_z = send(text, text_pairs)
        text_y = send(text, y_pairs)
        image_z = send(image, image_pairs)
        text_zy = send(text_z, y_pairs)
        texts = [text, text_z, text_y, text_zy]
        text_parts, image_part, loss_own, sums = tile(scalars, gains, shifts, image, texts)
        text_part, text_z_part, y_parts, image_z_part, sums = tile(
            scalars, gains, shifts, image_z, texts, [text_parts, sums]
        )

        image_back = send(image_z_part, image_pairs)
        y_back = send(y_parts, y_pairs)
        sums = sum_over(sums, early_steps, turns)
        sums, y_back = lax.optimization_barrier((sums, y_back))
        text_z_sum = text_z_part + y_back[:rows].astype(jnp.float32)
        text_z_back = send(text_z_sum.astype(jnp.bfloat16), text_pairs)
        sums = sum_over(sums, middle_steps, turns)
        sums, image_back, text_z_back = lax.optimization_barrier((sums, image_back, text_z_back))
        image_grad = backward_norm(
            image_feats[0], gains[:1], shifts[:1], scale, [(0, image_part), (0, image_back)]
        )
        sums = sums + send(sums, late_steps[0])
        sums, image_grad = lax.optimization_barrier((sums, image_grad))
        for pairs in late_steps[1:]:
            sums = sums + send(sums, pairs)
        text_grad = backward_norm(
            text_feats[0],
            gains[1:],
            shifts[1:],
            scale,
            [(0, text_part), (rows, y_back), (0, text_z_back)],
        )

        row_mean = (loss_own + get_line(image_back[rows:], rows)) / (group_rows * rows)
        return (image_grad[None], text_grad[None], sums[:2], sums[2:], row_mean)

    return body


def build(mesh, sizes):
    placed = (P("dp", "img", None), P("dp", "img", None), P(), P(), P(), P())
    return jax.shard_map(
        make_body(Routes(sizes)),
        mesh=mesh,
        in_specs=placed,
        out_specs=(P("dp", "img", None), P("dp", "img", None), P(), P(), P("dp", "img")),
        check_vma=False,
    )


def solution(mesh):
    y_high, cores = Y_HIGH, mesh.shape["dp"] // Y_HIGH
    y_low = mesh.shape["img"] // (RING * Z_BLOCK * X_CHIPS)
    return build(mesh, (y_low, RING, Z_BLOCK, X_CHIPS, y_high, cores))
```

```python
import functools

import jax
import jax.numpy as jnp
from jax import lax
from jax.experimental import pallas as pl
from jax.experimental.pallas import tpu as pltpu
from jax.sharding import PartitionSpec as P

AXES = ("img", "dp")
RING = 4
X_CHIPS = 4
Z_BLOCK = 4
Y_HIGH = 4

VMEM_LIMIT = 60 << 20
TILE_VMEM_LIMIT = 24 << 20
ROW_BLOCK = 16
UNROLL = 4
EPS = 1e-06
EXTRA = 16
LANES = 256
NT = (((1,), (1,)), ((), ()))
TN = (((0,), (0,)), ((), ()))


def to_lanes(column):
    count = column.shape[0]
    on = lax.broadcasted_iota(jnp.int32, (count, count), 0) == lax.broadcasted_iota(
        jnp.int32, (count, count), 1
    )
    return jnp.sum(jnp.where(on, column, 0.0), axis=0, keepdims=True)


def to_rows(line):
    count = line.shape[1]
    on = lax.broadcasted_iota(jnp.int32, (count, count), 0) == lax.broadcasted_iota(
        jnp.int32, (count, count), 1
    )
    return jnp.sum(jnp.where(on, line, 0.0), axis=1, keepdims=True)


def put_line(ref, line):
    count = line.shape[1]
    rows = ref.shape[0] - EXTRA
    ref[rows:, :] = jnp.zeros((EXTRA, ref.shape[1]), ref.dtype)
    for term in range(3):
        piece = line.astype(jnp.bfloat16)
        line = line - piece.astype(jnp.float32)
        ref[rows:, term * LANES : term * LANES + count] = jnp.broadcast_to(piece, (EXTRA, count))


def get_line(block, count):
    terms = [
        block[:1, term * LANES : term * LANES + count].astype(jnp.float32) for term in range(3)
    ]
    return terms[0] + (terms[1] + terms[2])


def norm_rows(feats, gain, shift):
    center = jnp.mean(feats, axis=-1, keepdims=True)
    offset = feats - center
    spread = jnp.mean(offset * offset, axis=-1, keepdims=True)
    rstd = lax.rsqrt(spread + EPS)
    normed = offset * rstd
    unnormed = normed * gain + shift
    inverse = lax.rsqrt(jnp.sum(unnormed * unnormed, axis=-1, keepdims=True) + EPS)
    return normed, rstd, unnormed, inverse


def forward_kernel(image_ref, text_ref, gains_ref, shifts_ref, image_emb_ref, text_emb_ref, keep):
    for tower, (feats_ref, emb_ref) in enumerate(
        ((image_ref, image_emb_ref), (text_ref, text_emb_ref))
    ):
        gain = gains_ref[tower : tower + 1, :]
        shift = shifts_ref[tower : tower + 1, :]

        @pl.loop(0, feats_ref.shape[0] // ROW_BLOCK, unroll=UNROLL)
        def _(step):
            rows = pl.ds(pl.multiple_of(step * ROW_BLOCK, ROW_BLOCK), ROW_BLOCK)
            feats = feats_ref[rows, :].astype(jnp.float32)
            _, _, unnormed, inverse = norm_rows(feats, gain, shift)
            emb_ref[rows, :] = (unnormed * inverse).astype(jnp.bfloat16)
            keep[rows, :] = jnp.broadcast_to(inverse, (ROW_BLOCK, 128))

        put_line(emb_ref, to_lanes(keep[:, :1]))


def forward_norms(image_feats, text_feats, gains, shifts):
    rows, width = image_feats.shape
    emb = jax.ShapeDtypeStruct((rows + EXTRA, width), jnp.bfloat16)
    return pl.pallas_call(
        forward_kernel,
        out_shape=(emb, emb),
        scratch_shapes=[pltpu.VMEM((rows, 128), jnp.float32)],
        compiler_params=pltpu.CompilerParams(vmem_limit_bytes=VMEM_LIMIT),
        cost_estimate=pl.CostEstimate(
            flops=40 * rows * width, bytes_accessed=8 * rows * width, transcendentals=0
        ),
        name="forward_norms",
    )(image_feats, text_feats, gains, shifts)


def add_sums(units, parts, inverses):
    along = jnp.sum(units * parts, axis=-1, keepdims=True)
    pulled = parts - units * along
    return (
        jnp.sum(units * pulled, axis=0, keepdims=True),
        jnp.sum(inverses * pulled, axis=0, keepdims=True),
    )


def tile_kernel(final, scalars_ref, gains_ref, shifts_ref, *refs):
    image_in, text_ins = refs[0], refs[1:5]
    if final:
        parts_before, sums_before = refs[5:7]
        text_ref, text_z_ref, texts_ref, image_ref, sums_ref = refs[7:12]
    else:
        parts_ref, image_ref, loss_ref, sums_ref = refs[5:9]
    texts, coeff = refs[-2:]
    rows = coeff.shape[0]
    image = image_in[:rows, :]
    for at, ref in enumerate(text_ins):
        texts[at * rows : (at + 1) * rows, :] = ref[:rows, :]
    logits = lax.dot_general(image, texts[...], NT, preferred_element_type=jnp.float32)
    logits = scalars_ref[0] * logits + scalars_ref[1]
    if not final:
        row_at = lax.broadcasted_iota(jnp.int32, logits.shape, 0)
        column_at = lax.broadcasted_iota(jnp.int32, logits.shape, 1)
        signs = jnp.where(row_at == column_at, -1.0, 1.0)
        logits = signs * logits
    small = jnp.exp(-jnp.abs(logits))
    terms = jnp.maximum(logits, 0.0) + jnp.log1p(small)
    slopes = jnp.where(logits >= 0.0, 1.0, small) / (1.0 + small)
    if not final:
        slopes = signs * slopes
    coeff[...] = slopes.astype(jnp.bfloat16)
    losses = to_lanes(jnp.sum(terms, axis=1, keepdims=True))
    if final:
        put_line(image_ref, losses)
    else:
        loss_ref[...] = losses

    unit_sum, shift_sum = 0.0, 0.0
    for at in (3, 2, 1, 0):
        own = slice(at * rows, (at + 1) * rows)
        part = lax.dot_general(coeff[:, own], image, TN, preferred_element_type=jnp.float32)
        if not final:
            parts_ref[own, :] = part
        elif at >= 2:
            whole = part + parts_before[own, :]
            texts_ref[(3 - at) * rows : (4 - at) * rows, :] = whole.astype(jnp.bfloat16)
        else:
            (text_ref, text_z_ref)[at][...] = part + parts_before[own, :]
        inverse = to_rows(get_line(text_ins[at][rows:, :], rows))
        unit_add, shift_add = add_sums(texts[own, :].astype(jnp.float32), part, inverse)
        unit_sum, shift_sum = unit_sum + unit_add, shift_sum + shift_add
    part = jnp.dot(coeff[...], texts[...], preferred_element_type=jnp.float32)
    if final:
        image_ref[:rows, :] = part.astype(jnp.bfloat16)
    else:
        image_ref[...] = part
    inverse = to_rows(get_line(image_in[rows:, :], rows))
    image_unit_sum, image_shift_sum = add_sums(image.astype(jnp.float32), part, inverse)
    sums = (image_unit_sum, unit_sum, image_shift_sum, shift_sum)
    if not final:
        for at in range(4):
            sums_ref[at : at + 1, :] = sums[at]
        return
    for tower in range(2):
        shift = shifts_ref[tower : tower + 1, :]
        unit_sum = sums[tower] + sums_before[tower : tower + 1, :]
        shift_sum = sums[2 + tower] + sums_before[2 + tower : 3 + tower, :]
        gain_sum = (unit_sum - shift * shift_sum) / gains_ref[tower : tower + 1, :]
        sums_ref[tower : tower + 1, :] = scalars_ref[0] * gain_sum
        sums_ref[2 + tower : 3 + tower, :] = scalars_ref[0] * shift_sum


def tile(scalars, gains, shifts, image, texts, before=()):
    rows, width = image.shape[0] - EXTRA, image.shape[1]
    final = len(before) > 0
    whole = pl.BlockSpec(memory_space=pltpu.VMEM)

    def wide(count, kind):
        return jax.ShapeDtypeStruct((count, width), kind)

    if final:
        outs = [wide(rows, jnp.float32)] * 2
        outs += [wide(2 * rows, jnp.bfloat16), wide(rows + EXTRA, jnp.bfloat16)]
    else:
        outs = [wide(4 * rows, jnp.float32), wide(rows, jnp.float32)]
        outs += [jax.ShapeDtypeStruct((1, rows), jnp.float32)]
    outs += [wide(4, jnp.float32)]
    return pl.pallas_call(
        functools.partial(tile_kernel, final),
        out_shape=tuple(outs),
        in_specs=[pl.BlockSpec(memory_space=pltpu.SMEM)] + [whole] * (7 + len(before)),
        out_specs=(whole,) * len(outs),
        scratch_shapes=[
            pltpu.VMEM((4 * rows, width), jnp.bfloat16),
            pltpu.VMEM((rows, 4 * rows), jnp.bfloat16),
        ],
        compiler_params=pltpu.CompilerParams(vmem_limit_bytes=TILE_VMEM_LIMIT),
        cost_estimate=pl.CostEstimate(
            flops=24 * rows * rows * width,
            bytes_accessed=24 * rows * width,
            transcendentals=12 * rows * rows,
        ),
        name="last_tile" if final else "first_tile",
    )(scalars, gains, shifts, image, *texts, *before)


def backward_kernel(firsts, feats_ref, gain_ref, shift_ref, scale_ref, *refs):
    count = len(firsts)
    part_refs = refs[:count]
    if len(refs) > count + 1:
        loss_ref, grad_ref, mean_ref = refs[count:]
        rows = loss_ref.shape[1]
        losses = loss_ref[...] + get_line(part_refs[-1][rows:, :], rows)
        mean_ref[...] = losses / (2 * RING * rows)
    else:
        grad_ref = refs[count]

    @pl.loop(0, feats_ref.shape[0] // ROW_BLOCK, unroll=UNROLL)
    def _(step):
        rows = pl.ds(pl.multiple_of(step * ROW_BLOCK, ROW_BLOCK), ROW_BLOCK)
        feats = feats_ref[rows, :].astype(jnp.float32)
        gain = gain_ref[...]
        normed, rstd, unnormed, inverse = norm_rows(feats, gain, shift_ref[...])
        unit = unnormed * inverse
        pulled = 0.0
        for first, part_ref in zip(firsts, part_refs):
            at = pl.ds(pl.multiple_of(first + step * ROW_BLOCK, ROW_BLOCK), ROW_BLOCK)
            pulled = pulled + part_ref[at, :].astype(jnp.float32)
        pulled = pulled * scale_ref[0]
        along = jnp.sum(unit * pulled, axis=-1, keepdims=True)
        pulled = inverse * (pulled - unit * along) * gain
        pulled = pulled - normed * jnp.mean(pulled * normed, axis=-1, keepdims=True)
        pulled = rstd * (pulled - jnp.mean(pulled, axis=-1, keepdims=True))
        grad_ref[rows, :] = pulled.astype(jnp.bfloat16)


def backward_norm(feats, gain, shift, scale, parts, loss=None):
    rows, width = feats.shape
    firsts = [first for first, _ in parts]
    values = [part for _, part in parts]
    whole = pl.BlockSpec(memory_space=pltpu.VMEM)
    out_shape = (jax.ShapeDtypeStruct((rows, width), jnp.bfloat16),)
    if loss is not None:
        values.append(loss)
        out_shape += (jax.ShapeDtypeStruct((1, rows), jnp.float32),)
    return pl.pallas_call(
        functools.partial(backward_kernel, firsts),
        out_shape=out_shape,
        in_specs=[whole] * 3 + [pl.BlockSpec(memory_space=pltpu.SMEM)] + [whole] * len(values),
        out_specs=(whole,) * len(out_shape),
        compiler_params=pltpu.CompilerParams(vmem_limit_bytes=VMEM_LIMIT),
        cost_estimate=pl.CostEstimate(
            flops=40 * rows * width, bytes_accessed=12 * rows * width, transcendentals=0
        ),
        name="backward_norm",
    )(feats, gain, shift, scale, *values)


def near(place):
    return place ^ 1


def far(place):
    return RING - 1 - place


class Routes:
    def __init__(self, sizes):
        self.sizes = sizes
        y_lo, z_hi, z_lo, x, y_hi, core = sizes
        self.count = y_lo * z_hi * z_lo * x * y_hi * core

    def split(self, index):
        place = []
        for size in reversed(self.sizes):
            place.append(index % size)
            index //= size
        return place[::-1]

    def join(self, place):
        index = 0
        for size, at in zip(self.sizes, place):
            index = index * size + at
        return index

    def pairs(self, move):
        out = []
        for index in range(self.count):
            place = self.split(index)
            out.append((index, self.join(move(list(place)))))
        return out

    def along(self, axis, step):
        def move(place):
            place[axis] = step(place[axis])
            return place

        return self.pairs(move)

    def across_y(self):
        return self.along(0, near)

    def towers(self):
        def text(place):
            place[1] = far(place[1]) if place[5] == 0 else near(place[1])
            return place

        def image(place):
            place[1] = near(place[1]) if place[5] == 0 else far(place[1])
            return place

        return self.pairs(text), self.pairs(image)

    def ring(self, high, low):
        size = self.sizes[low] * (1 if high is None else self.sizes[high])
        steps = []
        reach = -1
        while 2 ** len(steps) < size:

            def move(place, reach=reach):
                at = place[low] + (0 if high is None else place[high] * self.sizes[low])
                at = (at + (reach if at % 2 else -reach)) % size
                place[low] = at % self.sizes[low]
                if high is not None:
                    place[high] = at // self.sizes[low]
                return place

            steps.append(self.pairs(move))
            reach = -2 * reach - 1
        return steps


def send(value, pairs):
    return lax.ppermute(value, AXES, pairs)


def once(step, value, turns):
    return lax.while_loop(
        lambda carry: carry[0] < turns,
        lambda carry: (carry[0] + 1, step(carry[1])),
        (jnp.int32(0), value),
    )[1]


def sum_over(value, steps):
    for pairs in steps:
        value = value + send(value, pairs)
    return value


def make_body(routes):
    text_pairs, image_pairs = routes.towers()
    y_pairs = routes.across_y()
    z_steps = routes.ring(1, 2)
    flat_steps = [routes.along(5, near), *routes.ring(None, 3), *routes.ring(4, 0)]
    early_steps, middle_steps = flat_steps[:4], flat_steps[4:] + z_steps[:-2]
    late_steps = z_steps[-2:]

    def body(image_feats, text_feats, gains, shifts, log_scale, logit_bias):
        scale = jnp.exp(log_scale)
        scalars = jnp.concatenate([scale, logit_bias])
        turns = jnp.where(log_scale[0] == log_scale[0], 1, 0)
        image, text = forward_norms(image_feats[0], text_feats[0], gains, shifts)
        rows = image_feats.shape[1]

        text_z = send(text, text_pairs)
        text_y = send(text, y_pairs)
        image_late, text_z = lax.optimization_barrier((image, text_z))
        image_z = send(image_late, image_pairs)
        text_zy = once(lambda block: send(block, y_pairs), text_z, turns)
        texts = [text, text_z, text_y, text_zy]
        text_parts, image_part, loss_own, sums = tile(scalars, gains, shifts, image, texts)
        text_part, text_z_part, y_parts, image_z_part, sums = tile(
            scalars, gains, shifts, image_z, texts, [text_parts, sums]
        )

        image_back = send(image_z_part, image_pairs)
        y_back = send(y_parts, y_pairs)
        sums = once(lambda value: sum_over(value, early_steps), sums, turns)
        sums, y_back = lax.optimization_barrier((sums, y_back))
        text_z_sum = text_z_part + y_back[:rows].astype(jnp.float32)
        text_z_back = send(text_z_sum.astype(jnp.bfloat16), text_pairs)
        sums = once(lambda value: sum_over(value, middle_steps), sums, turns)
        sums, image_back, text_z_back = lax.optimization_barrier((sums, image_back, text_z_back))
        image_grad, row_mean = backward_norm(
            image_feats[0],
            gains[:1],
            shifts[:1],
            scale,
            [(0, image_part), (0, image_back)],
            loss_own,
        )
        sums = sums + send(sums, late_steps[0])
        sums, image_grad = lax.optimization_barrier((sums, image_grad))
        for pairs in late_steps[1:]:
            sums = sums + send(sums, pairs)
        (text_grad,) = backward_norm(
            text_feats[0],
            gains[1:],
            shifts[1:],
            scale,
            [(0, text_part), (rows, y_back), (0, text_z_back)],
        )
        return (image_grad[None], text_grad[None], sums[:2], sums[2:], row_mean)

    return body


def build(mesh, sizes):
    placed = (P("dp", "img", None), P("dp", "img", None), P(), P(), P(), P())
    return jax.shard_map(
        make_body(Routes(sizes)),
        mesh=mesh,
        in_specs=placed,
        out_specs=(P("dp", "img", None), P("dp", "img", None), P(), P(), P("dp", "img")),
        check_vma=False,
    )


def solution(mesh):
    y_high, cores = Y_HIGH, mesh.shape["dp"] // Y_HIGH
    y_low = mesh.shape["img"] // (RING * Z_BLOCK * X_CHIPS)
    return build(mesh, (y_low, RING, Z_BLOCK, X_CHIPS, y_high, cores))
```

```python
import functools

import jax
import jax.numpy as jnp
from jax import lax
from jax.experimental import pallas as pl
from jax.experimental.pallas import tpu as pltpu
from jax.sharding import PartitionSpec as P

AXES = ("img", "dp")
RING = 4
X_CHIPS = 4
Z_BLOCK = 4
Y_HIGH = 4

VMEM_LIMIT = 60 << 20
TILE_VMEM_LIMIT = 24 << 20
ROW_BLOCK = 16
UNROLL = 4
EPS = 1e-06
EXTRA = 8
LANES = 256
NT = (((1,), (1,)), ((), ()))
TN = (((0,), (0,)), ((), ()))


def to_lanes(column):
    count = column.shape[0]
    on = lax.broadcasted_iota(jnp.int32, (count, count), 0) == lax.broadcasted_iota(
        jnp.int32, (count, count), 1
    )
    return jnp.sum(jnp.where(on, column, 0.0), axis=0, keepdims=True)


def to_rows(line):
    count = line.shape[1]
    on = lax.broadcasted_iota(jnp.int32, (count, count), 0) == lax.broadcasted_iota(
        jnp.int32, (count, count), 1
    )
    return jnp.sum(jnp.where(on, line, 0.0), axis=1, keepdims=True)


def put_line(ref, line):
    count = line.shape[1]
    rows = ref.shape[0] - EXTRA
    ref[rows:, :] = jnp.zeros((EXTRA, ref.shape[1]), ref.dtype)
    for term in range(3):
        piece = line.astype(jnp.bfloat16)
        line = line - piece.astype(jnp.float32)
        ref[rows:, term * LANES : term * LANES + count] = jnp.broadcast_to(piece, (EXTRA, count))


def get_line(block, count):
    terms = [
        block[:1, term * LANES : term * LANES + count].astype(jnp.float32) for term in range(3)
    ]
    return terms[0] + (terms[1] + terms[2])


def norm_rows(feats, gain, shift):
    center = jnp.mean(feats, axis=-1, keepdims=True)
    offset = feats - center
    spread = jnp.mean(offset * offset, axis=-1, keepdims=True)
    rstd = lax.rsqrt(spread + EPS)
    normed = offset * rstd
    unnormed = normed * gain + shift
    inverse = lax.rsqrt(jnp.sum(unnormed * unnormed, axis=-1, keepdims=True) + EPS)
    return normed, rstd, unnormed, inverse


def forward_kernel(image_ref, text_ref, gains_ref, shifts_ref, image_emb_ref, text_emb_ref, keep):
    for tower, (feats_ref, emb_ref) in enumerate(
        ((image_ref, image_emb_ref), (text_ref, text_emb_ref))
    ):
        gain = gains_ref[tower : tower + 1, :]
        shift = shifts_ref[tower : tower + 1, :]

        @pl.loop(0, feats_ref.shape[0] // ROW_BLOCK, unroll=UNROLL)
        def _(step):
            rows = pl.ds(pl.multiple_of(step * ROW_BLOCK, ROW_BLOCK), ROW_BLOCK)
            feats = feats_ref[rows, :].astype(jnp.float32)
            _, _, unnormed, inverse = norm_rows(feats, gain, shift)
            emb_ref[rows, :] = (unnormed * inverse).astype(jnp.bfloat16)
            keep[rows, :] = jnp.broadcast_to(inverse, (ROW_BLOCK, 128))

        put_line(emb_ref, to_lanes(keep[:, :1]))


def forward_norms(image_feats, text_feats, gains, shifts):
    rows, width = image_feats.shape
    emb = jax.ShapeDtypeStruct((rows + EXTRA, width), jnp.bfloat16)
    return pl.pallas_call(
        forward_kernel,
        out_shape=(emb, emb),
        scratch_shapes=[pltpu.VMEM((rows, 128), jnp.float32)],
        compiler_params=pltpu.CompilerParams(vmem_limit_bytes=VMEM_LIMIT),
        cost_estimate=pl.CostEstimate(
            flops=40 * rows * width, bytes_accessed=8 * rows * width, transcendentals=0
        ),
        name="forward_norms",
    )(image_feats, text_feats, gains, shifts)


def add_sums(units, parts, inverses):
    along = jnp.sum(units * parts, axis=-1, keepdims=True)
    pulled = parts - units * along
    return (
        jnp.sum(units * pulled, axis=0, keepdims=True),
        jnp.sum(inverses * pulled, axis=0, keepdims=True),
    )


def tile_kernel(final, scalars_ref, gains_ref, shifts_ref, *refs):
    image_in, text_ins = refs[0], refs[1:5]
    if final:
        parts_before, sums_before = refs[5:7]
        text_ref, text_z_ref, texts_ref, image_ref, sums_ref = refs[7:12]
    else:
        parts_ref, image_ref, loss_ref, sums_ref = refs[5:9]
    texts, coeff = refs[-2:]
    rows = coeff.shape[0]
    image = image_in[:rows, :]
    for at, ref in enumerate(text_ins):
        texts[at * rows : (at + 1) * rows, :] = ref[:rows, :]
    logits = lax.dot_general(image, texts[...], NT, preferred_element_type=jnp.float32)
    logits = scalars_ref[0] * logits + scalars_ref[1]
    if not final:
        row_at = lax.broadcasted_iota(jnp.int32, logits.shape, 0)
        column_at = lax.broadcasted_iota(jnp.int32, logits.shape, 1)
        signs = jnp.where(row_at == column_at, -1.0, 1.0)
        logits = signs * logits
    small = jnp.exp(-jnp.abs(logits))
    terms = jnp.maximum(logits, 0.0) + jnp.log1p(small)
    slopes = jnp.where(logits >= 0.0, 1.0, small) / (1.0 + small)
    if not final:
        slopes = signs * slopes
    coeff[...] = slopes.astype(jnp.bfloat16)
    losses = to_lanes(jnp.sum(terms, axis=1, keepdims=True))
    if final:
        put_line(image_ref, losses)
    else:
        loss_ref[...] = losses

    unit_sum, shift_sum = 0.0, 0.0
    for at in (3, 2, 1, 0):
        own = slice(at * rows, (at + 1) * rows)
        part = lax.dot_general(coeff[:, own], image, TN, preferred_element_type=jnp.float32)
        if not final:
            parts_ref[own, :] = part
        elif at >= 2:
            whole = part + parts_before[own, :]
            texts_ref[(3 - at) * rows : (4 - at) * rows, :] = whole.astype(jnp.bfloat16)
        else:
            (text_ref, text_z_ref)[at][...] = part + parts_before[own, :]
        inverse = to_rows(get_line(text_ins[at][rows:, :], rows))
        unit_add, shift_add = add_sums(texts[own, :].astype(jnp.float32), part, inverse)
        unit_sum, shift_sum = unit_sum + unit_add, shift_sum + shift_add
    part = jnp.dot(coeff[...], texts[...], preferred_element_type=jnp.float32)
    if final:
        image_ref[:rows, :] = part.astype(jnp.bfloat16)
    else:
        image_ref[...] = part
    inverse = to_rows(get_line(image_in[rows:, :], rows))
    image_unit_sum, image_shift_sum = add_sums(image.astype(jnp.float32), part, inverse)
    sums = (image_unit_sum, unit_sum, image_shift_sum, shift_sum)
    if not final:
        for at in range(4):
            sums_ref[at : at + 1, :] = sums[at]
        return
    for tower in range(2):
        shift = shifts_ref[tower : tower + 1, :]
        unit_sum = sums[tower] + sums_before[tower : tower + 1, :]
        shift_sum = sums[2 + tower] + sums_before[2 + tower : 3 + tower, :]
        gain_sum = (unit_sum - shift * shift_sum) / gains_ref[tower : tower + 1, :]
        sums_ref[tower : tower + 1, :] = scalars_ref[0] * gain_sum
        sums_ref[2 + tower : 3 + tower, :] = scalars_ref[0] * shift_sum


def tile(scalars, gains, shifts, image, texts, before=()):
    rows, width = image.shape[0] - EXTRA, image.shape[1]
    final = len(before) > 0
    whole = pl.BlockSpec(memory_space=pltpu.VMEM)

    def wide(count, kind):
        return jax.ShapeDtypeStruct((count, width), kind)

    if final:
        outs = [wide(rows, jnp.float32)] * 2
        outs += [wide(2 * rows, jnp.bfloat16), wide(rows + EXTRA, jnp.bfloat16)]
    else:
        outs = [wide(4 * rows, jnp.float32), wide(rows, jnp.float32)]
        outs += [jax.ShapeDtypeStruct((1, rows), jnp.float32)]
    outs += [wide(4, jnp.float32)]
    return pl.pallas_call(
        functools.partial(tile_kernel, final),
        out_shape=tuple(outs),
        in_specs=[pl.BlockSpec(memory_space=pltpu.SMEM)] + [whole] * (7 + len(before)),
        out_specs=(whole,) * len(outs),
        scratch_shapes=[
            pltpu.VMEM((4 * rows, width), jnp.bfloat16),
            pltpu.VMEM((rows, 4 * rows), jnp.bfloat16),
        ],
        compiler_params=pltpu.CompilerParams(vmem_limit_bytes=TILE_VMEM_LIMIT),
        cost_estimate=pl.CostEstimate(
            flops=24 * rows * rows * width,
            bytes_accessed=24 * rows * width,
            transcendentals=12 * rows * rows,
        ),
        name="last_tile" if final else "first_tile",
    )(scalars, gains, shifts, image, *texts, *before)


def backward_kernel(tower, firsts, feats_ref, gains_ref, shifts_ref, scale_ref, *refs):
    count = len(firsts)
    part_refs = refs[:count]
    if len(refs) > count + 1:
        loss_ref, grad_ref, mean_ref = refs[count:]
        rows = loss_ref.shape[1]
        losses = loss_ref[...] + get_line(part_refs[-1][rows:, :], rows)
        mean_ref[...] = losses / (2 * RING * rows)
    else:
        grad_ref = refs[count]

    @pl.loop(0, feats_ref.shape[0] // ROW_BLOCK, unroll=True)
    def _(step):
        rows = pl.ds(pl.multiple_of(step * ROW_BLOCK, ROW_BLOCK), ROW_BLOCK)
        feats = feats_ref[rows, :].astype(jnp.float32)
        gain = gains_ref[tower : tower + 1, :]
        shift = shifts_ref[tower : tower + 1, :]
        normed, rstd, unnormed, inverse = norm_rows(feats, gain, shift)
        unit = unnormed * inverse
        pulled = 0.0
        for first, part_ref in zip(firsts, part_refs):
            at = pl.ds(pl.multiple_of(first + step * ROW_BLOCK, ROW_BLOCK), ROW_BLOCK)
            pulled = pulled + part_ref[at, :].astype(jnp.float32)
        pulled = pulled * scale_ref[0]
        along = jnp.sum(unit * pulled, axis=-1, keepdims=True)
        pulled = inverse * (pulled - unit * along) * gain
        pulled = pulled - normed * jnp.mean(pulled * normed, axis=-1, keepdims=True)
        pulled = rstd * (pulled - jnp.mean(pulled, axis=-1, keepdims=True))
        grad_ref[rows, :] = pulled.astype(jnp.bfloat16)


def backward_norm(tower, feats, gains, shifts, scale, parts, loss=None):
    rows, width = feats.shape
    firsts = [first for first, _ in parts]
    values = [part for _, part in parts]
    whole = pl.BlockSpec(memory_space=pltpu.VMEM)
    out_shape = (jax.ShapeDtypeStruct((rows, width), jnp.bfloat16),)
    if loss is not None:
        values.append(loss)
        out_shape += (jax.ShapeDtypeStruct((1, rows), jnp.float32),)
    return pl.pallas_call(
        functools.partial(backward_kernel, tower, firsts),
        out_shape=out_shape,
        in_specs=[whole] * 3 + [pl.BlockSpec(memory_space=pltpu.SMEM)] + [whole] * len(values),
        out_specs=(whole,) * len(out_shape),
        compiler_params=pltpu.CompilerParams(vmem_limit_bytes=VMEM_LIMIT),
        cost_estimate=pl.CostEstimate(
            flops=40 * rows * width, bytes_accessed=12 * rows * width, transcendentals=0
        ),
        name="backward_norm",
    )(feats, gains, shifts, scale, *values)


def near(place):
    return place ^ 1


def far(place):
    return RING - 1 - place


class Routes:
    def __init__(self, sizes):
        self.sizes = sizes
        y_lo, z_hi, z_lo, x, y_hi, core = sizes
        self.count = y_lo * z_hi * z_lo * x * y_hi * core

    def split(self, index):
        place = []
        for size in reversed(self.sizes):
            place.append(index % size)
            index //= size
        return place[::-1]

    def join(self, place):
        index = 0
        for size, at in zip(self.sizes, place):
            index = index * size + at
        return index

    def pairs(self, move):
        out = []
        for index in range(self.count):
            place = self.split(index)
            out.append((index, self.join(move(list(place)))))
        return out

    def along(self, axis, step):
        def move(place):
            place[axis] = step(place[axis])
            return place

        return self.pairs(move)

    def across_y(self):
        return self.along(0, near)

    def towers(self):
        def text(place):
            place[1] = far(place[1]) if place[5] == 0 else near(place[1])
            return place

        def image(place):
            place[1] = near(place[1]) if place[5] == 0 else far(place[1])
            return place

        return self.pairs(text), self.pairs(image)

    def ring(self, high, low):
        size = self.sizes[low] * (1 if high is None else self.sizes[high])
        steps = []
        reach = -1
        while 2 ** len(steps) < size:

            def move(place, reach=reach):
                at = place[low] + (0 if high is None else place[high] * self.sizes[low])
                at = (at + (reach if at % 2 else -reach)) % size
                place[low] = at % self.sizes[low]
                if high is not None:
                    place[high] = at // self.sizes[low]
                return place

            steps.append(self.pairs(move))
            reach = -2 * reach - 1
        return steps


def send(value, pairs):
    return lax.ppermute(value, AXES, pairs)


def once(step, value, turns):
    return lax.while_loop(
        lambda carry: carry[0] < turns,
        lambda carry: (carry[0] + 1, step(carry[1])),
        (jnp.int32(0), value),
    )[1]


def sum_over(value, steps):
    for pairs in steps:
        value = value + send(value, pairs)
    return value


def make_body(routes):
    text_pairs, image_pairs = routes.towers()
    y_pairs = routes.across_y()
    z_steps = routes.ring(1, 2)
    flat_steps = [routes.along(5, near), *routes.ring(None, 3), *routes.ring(4, 0)]
    early_steps, middle_steps = flat_steps[:4], flat_steps[4:] + z_steps[:-2]
    late_steps = z_steps[-2:]

    def body(image_feats, text_feats, gains, shifts, log_scale, logit_bias):
        scale = jnp.exp(log_scale)
        scalars = jnp.concatenate([scale, logit_bias])
        turns = jnp.where(log_scale[0] == log_scale[0], 1, 0)
        image, text = forward_norms(image_feats[0], text_feats[0], gains, shifts)
        rows = image_feats.shape[1]

        text_z = send(text, text_pairs)
        text_y = send(text, y_pairs)
        image_late, text_z = lax.optimization_barrier((image, text_z))
        image_z = send(image_late, image_pairs)
        text_zy = once(lambda block: send(block, y_pairs), text_z, turns)
        texts = [text, text_z, text_y, text_zy]
        text_parts, image_part, loss_own, sums = tile(scalars, gains, shifts, image, texts)
        text_part, text_z_part, y_parts, image_z_part, sums = tile(
            scalars, gains, shifts, image_z, texts, [text_parts, sums]
        )

        image_back = send(image_z_part, image_pairs)
        y_back = send(y_parts, y_pairs)
        sums = once(lambda value: sum_over(value, early_steps), sums, turns)
        sums, y_back = lax.optimization_barrier((sums, y_back))
        text_z_sum = text_z_part + y_back[:rows].astype(jnp.float32)
        text_z_back = send(text_z_sum.astype(jnp.bfloat16), text_pairs)
        sums = once(lambda value: sum_over(value, middle_steps), sums, turns)
        sums, image_back, text_z_back = lax.optimization_barrier((sums, image_back, text_z_back))
        image_grad, row_mean = backward_norm(
            0,
            image_feats[0],
            gains,
            shifts,
            scale,
            [(0, image_part), (0, image_back)],
            loss_own,
        )
        sums = sums + send(sums, late_steps[0])
        sums, image_grad = lax.optimization_barrier((sums, image_grad))
        for pairs in late_steps[1:]:
            sums = sums + send(sums, pairs)
        (text_grad,) = backward_norm(
            1,
            text_feats[0],
            gains,
            shifts,
            scale,
            [(0, text_part), (rows, y_back), (0, text_z_back)],
        )
        return (image_grad[None], text_grad[None], sums[:2], sums[2:], row_mean)

    return body


def build(mesh, sizes):
    placed = (P("dp", "img", None), P("dp", "img", None), P(), P(), P(), P())
    return jax.shard_map(
        make_body(Routes(sizes)),
        mesh=mesh,
        in_specs=placed,
        out_specs=(P("dp", "img", None), P("dp", "img", None), P(), P(), P("dp", "img")),
        check_vma=False,
    )


def solution(mesh):
    y_high, cores = Y_HIGH, mesh.shape["dp"] // Y_HIGH
    y_low = mesh.shape["img"] // (RING * Z_BLOCK * X_CHIPS)
    return build(mesh, (y_low, RING, Z_BLOCK, X_CHIPS, y_high, cores))
```

```python
import functools

import jax
import jax.numpy as jnp
from jax import lax
from jax.experimental import pallas as pl
from jax.experimental.pallas import tpu as pltpu
from jax.sharding import PartitionSpec as P

AXES = ("img", "dp")
RING = 4
X_CHIPS = 4
Z_BLOCK = 4
Y_HIGH = 4

VMEM_LIMIT = 60 << 20
TILE_VMEM_LIMIT = 24 << 20
ROW_BLOCK = 16
UNROLL = 4
EPS = 1e-06
EXTRA = 8
LANES = 256
NT = (((1,), (1,)), ((), ()))
TN = (((0,), (0,)), ((), ()))


def to_lanes(column):
    count = column.shape[0]
    on = lax.broadcasted_iota(jnp.int32, (count, count), 0) == lax.broadcasted_iota(
        jnp.int32, (count, count), 1
    )
    return jnp.sum(jnp.where(on, column, 0.0), axis=0, keepdims=True)


def to_rows(line):
    count = line.shape[1]
    on = lax.broadcasted_iota(jnp.int32, (count, count), 0) == lax.broadcasted_iota(
        jnp.int32, (count, count), 1
    )
    return jnp.sum(jnp.where(on, line, 0.0), axis=1, keepdims=True)


def put_line(ref, line):
    count = line.shape[1]
    rows = ref.shape[0] - EXTRA
    ref[rows:, :] = jnp.zeros((EXTRA, ref.shape[1]), ref.dtype)
    for term in range(3):
        piece = line.astype(jnp.bfloat16)
        line = line - piece.astype(jnp.float32)
        ref[rows:, term * LANES : term * LANES + count] = jnp.broadcast_to(piece, (EXTRA, count))


def get_line(block, count):
    terms = [
        block[:1, term * LANES : term * LANES + count].astype(jnp.float32) for term in range(3)
    ]
    return terms[0] + (terms[1] + terms[2])


def norm_rows(feats, gain, shift):
    center = jnp.mean(feats, axis=-1, keepdims=True)
    offset = feats - center
    spread = jnp.mean(offset * offset, axis=-1, keepdims=True)
    rstd = lax.rsqrt(spread + EPS)
    normed = offset * rstd
    unnormed = normed * gain + shift
    inverse = lax.rsqrt(jnp.sum(unnormed * unnormed, axis=-1, keepdims=True) + EPS)
    return normed, rstd, unnormed, inverse


def forward_kernel(tower, feats_ref, gains_ref, shifts_ref, emb_ref, keep):
    gain = gains_ref[tower : tower + 1, :]
    shift = shifts_ref[tower : tower + 1, :]

    @pl.loop(0, feats_ref.shape[0] // ROW_BLOCK, unroll=UNROLL)
    def _(step):
        rows = pl.ds(pl.multiple_of(step * ROW_BLOCK, ROW_BLOCK), ROW_BLOCK)
        feats = feats_ref[rows, :].astype(jnp.float32)
        _, _, unnormed, inverse = norm_rows(feats, gain, shift)
        emb_ref[rows, :] = (unnormed * inverse).astype(jnp.bfloat16)
        keep[rows, :] = jnp.broadcast_to(inverse, (ROW_BLOCK, 128))

    put_line(emb_ref, to_lanes(keep[:, :1]))


def forward_norm(tower, feats, gains, shifts):
    rows, width = feats.shape
    return pl.pallas_call(
        functools.partial(forward_kernel, tower),
        out_shape=jax.ShapeDtypeStruct((rows + EXTRA, width), jnp.bfloat16),
        scratch_shapes=[pltpu.VMEM((rows, 128), jnp.float32)],
        compiler_params=pltpu.CompilerParams(vmem_limit_bytes=VMEM_LIMIT),
        cost_estimate=pl.CostEstimate(
            flops=20 * rows * width, bytes_accessed=4 * rows * width, transcendentals=0
        ),
        name="forward_norm",
    )(feats, gains, shifts)


def add_sums(units, parts, inverses):
    along = jnp.sum(units * parts, axis=-1, keepdims=True)
    pulled = parts - units * along
    return (
        jnp.sum(units * pulled, axis=0, keepdims=True),
        jnp.sum(inverses * pulled, axis=0, keepdims=True),
    )


def tile_kernel(final, scalars_ref, gains_ref, shifts_ref, *refs):
    image_in, text_ins = refs[0], refs[1:5]
    if final:
        parts_before, sums_before = refs[5:7]
        text_ref, text_z_ref, texts_ref, image_ref, sums_ref = refs[7:12]
    else:
        parts_ref, image_ref, loss_ref, sums_ref = refs[5:9]
    texts, coeff = refs[-2:]
    rows = coeff.shape[0]
    image = image_in[:rows, :]
    for at, ref in enumerate(text_ins):
        texts[at * rows : (at + 1) * rows, :] = ref[:rows, :]
    logits = lax.dot_general(image, texts[...], NT, preferred_element_type=jnp.float32)
    logits = scalars_ref[0] * logits + scalars_ref[1]
    if not final:
        row_at = lax.broadcasted_iota(jnp.int32, logits.shape, 0)
        column_at = lax.broadcasted_iota(jnp.int32, logits.shape, 1)
        signs = jnp.where(row_at == column_at, -1.0, 1.0)
        logits = signs * logits
    small = jnp.exp(-jnp.abs(logits))
    terms = jnp.maximum(logits, 0.0) + jnp.log1p(small)
    slopes = jnp.where(logits >= 0.0, 1.0, small) / (1.0 + small)
    if not final:
        slopes = signs * slopes
    coeff[...] = slopes.astype(jnp.bfloat16)
    losses = to_lanes(jnp.sum(terms, axis=1, keepdims=True))
    if final:
        put_line(image_ref, losses)
    else:
        loss_ref[...] = losses

    unit_sum, shift_sum = 0.0, 0.0
    for at in (3, 2, 1, 0):
        own = slice(at * rows, (at + 1) * rows)
        part = lax.dot_general(coeff[:, own], image, TN, preferred_element_type=jnp.float32)
        if not final:
            parts_ref[own, :] = part
        elif at >= 2:
            whole = part + parts_before[own, :]
            texts_ref[(3 - at) * rows : (4 - at) * rows, :] = whole.astype(jnp.bfloat16)
        else:
            (text_ref, text_z_ref)[at][...] = part + parts_before[own, :]
        inverse = to_rows(get_line(text_ins[at][rows:, :], rows))
        unit_add, shift_add = add_sums(texts[own, :].astype(jnp.float32), part, inverse)
        unit_sum, shift_sum = unit_sum + unit_add, shift_sum + shift_add
    part = jnp.dot(coeff[...], texts[...], preferred_element_type=jnp.float32)
    if final:
        image_ref[:rows, :] = part.astype(jnp.bfloat16)
    else:
        image_ref[...] = part
    inverse = to_rows(get_line(image_in[rows:, :], rows))
    image_unit_sum, image_shift_sum = add_sums(image.astype(jnp.float32), part, inverse)
    sums = (image_unit_sum, unit_sum, image_shift_sum, shift_sum)
    if not final:
        for at in range(4):
            sums_ref[at : at + 1, :] = sums[at]
        return
    for tower in range(2):
        shift = shifts_ref[tower : tower + 1, :]
        unit_sum = sums[tower] + sums_before[tower : tower + 1, :]
        shift_sum = sums[2 + tower] + sums_before[2 + tower : 3 + tower, :]
        gain_sum = (unit_sum - shift * shift_sum) / gains_ref[tower : tower + 1, :]
        sums_ref[tower : tower + 1, :] = scalars_ref[0] * gain_sum
        sums_ref[2 + tower : 3 + tower, :] = scalars_ref[0] * shift_sum


def tile(scalars, gains, shifts, image, texts, before=()):
    rows, width = image.shape[0] - EXTRA, image.shape[1]
    final = len(before) > 0
    whole = pl.BlockSpec(memory_space=pltpu.VMEM)

    def wide(count, kind):
        return jax.ShapeDtypeStruct((count, width), kind)

    if final:
        outs = [wide(rows, jnp.float32)] * 2
        outs += [wide(2 * rows, jnp.bfloat16), wide(rows + EXTRA, jnp.bfloat16)]
    else:
        outs = [wide(4 * rows, jnp.float32), wide(rows, jnp.float32)]
        outs += [jax.ShapeDtypeStruct((1, rows), jnp.float32)]
    outs += [wide(4, jnp.float32)]
    return pl.pallas_call(
        functools.partial(tile_kernel, final),
        out_shape=tuple(outs),
        in_specs=[pl.BlockSpec(memory_space=pltpu.SMEM)] + [whole] * (7 + len(before)),
        out_specs=(whole,) * len(outs),
        scratch_shapes=[
            pltpu.VMEM((4 * rows, width), jnp.bfloat16),
            pltpu.VMEM((rows, 4 * rows), jnp.bfloat16),
        ],
        compiler_params=pltpu.CompilerParams(vmem_limit_bytes=TILE_VMEM_LIMIT),
        cost_estimate=pl.CostEstimate(
            flops=24 * rows * rows * width,
            bytes_accessed=24 * rows * width,
            transcendentals=12 * rows * rows,
        ),
        name="last_tile" if final else "first_tile",
    )(scalars, gains, shifts, image, *texts, *before)


def backward_kernel(tower, firsts, feats_ref, gains_ref, shifts_ref, scale_ref, *refs):
    count = len(firsts)
    part_refs = refs[:count]
    if len(refs) > count + 1:
        loss_ref, grad_ref, mean_ref = refs[count:]
        rows = loss_ref.shape[1]
        losses = loss_ref[...] + get_line(part_refs[-1][rows:, :], rows)
        mean_ref[...] = losses / (2 * RING * rows)
    else:
        grad_ref = refs[count]

    @pl.loop(0, feats_ref.shape[0] // ROW_BLOCK, unroll=True)
    def _(step):
        rows = pl.ds(pl.multiple_of(step * ROW_BLOCK, ROW_BLOCK), ROW_BLOCK)
        feats = feats_ref[rows, :].astype(jnp.float32)
        gain = gains_ref[tower : tower + 1, :]
        shift = shifts_ref[tower : tower + 1, :]
        normed, rstd, unnormed, inverse = norm_rows(feats, gain, shift)
        unit = unnormed * inverse
        pulled = 0.0
        for first, part_ref in zip(firsts, part_refs):
            at = pl.ds(pl.multiple_of(first + step * ROW_BLOCK, ROW_BLOCK), ROW_BLOCK)
            pulled = pulled + part_ref[at, :].astype(jnp.float32)
        pulled = pulled * scale_ref[0]
        along = jnp.sum(unit * pulled, axis=-1, keepdims=True)
        pulled = inverse * (pulled - unit * along) * gain
        pulled = pulled - normed * jnp.mean(pulled * normed, axis=-1, keepdims=True)
        pulled = rstd * (pulled - jnp.mean(pulled, axis=-1, keepdims=True))
        grad_ref[rows, :] = pulled.astype(jnp.bfloat16)


def backward_norm(tower, feats, gains, shifts, scale, parts, loss=None):
    rows, width = feats.shape
    firsts = [first for first, _ in parts]
    values = [part for _, part in parts]
    whole = pl.BlockSpec(memory_space=pltpu.VMEM)
    out_shape = (jax.ShapeDtypeStruct((rows, width), jnp.bfloat16),)
    if loss is not None:
        values.append(loss)
        out_shape += (jax.ShapeDtypeStruct((1, rows), jnp.float32),)
    return pl.pallas_call(
        functools.partial(backward_kernel, tower, firsts),
        out_shape=out_shape,
        in_specs=[whole] * 3 + [pl.BlockSpec(memory_space=pltpu.SMEM)] + [whole] * len(values),
        out_specs=(whole,) * len(out_shape),
        compiler_params=pltpu.CompilerParams(vmem_limit_bytes=VMEM_LIMIT),
        cost_estimate=pl.CostEstimate(
            flops=40 * rows * width, bytes_accessed=12 * rows * width, transcendentals=0
        ),
        name="backward_norm",
    )(feats, gains, shifts, scale, *values)


def near(place):
    return place ^ 1


def far(place):
    return RING - 1 - place


class Routes:
    def __init__(self, sizes):
        self.sizes = sizes
        y_lo, z_hi, z_lo, x, y_hi, core = sizes
        self.count = y_lo * z_hi * z_lo * x * y_hi * core

    def split(self, index):
        place = []
        for size in reversed(self.sizes):
            place.append(index % size)
            index //= size
        return place[::-1]

    def join(self, place):
        index = 0
        for size, at in zip(self.sizes, place):
            index = index * size + at
        return index

    def pairs(self, move):
        out = []
        for index in range(self.count):
            place = self.split(index)
            out.append((index, self.join(move(list(place)))))
        return out

    def along(self, axis, step):
        def move(place):
            place[axis] = step(place[axis])
            return place

        return self.pairs(move)

    def across_y(self):
        return self.along(0, near)

    def towers(self):
        def text(place):
            place[1] = far(place[1]) if place[5] == 0 else near(place[1])
            return place

        def image(place):
            place[1] = near(place[1]) if place[5] == 0 else far(place[1])
            return place

        return self.pairs(text), self.pairs(image)

    def ring(self, high, low):
        size = self.sizes[low] * (1 if high is None else self.sizes[high])
        steps = []
        reach = -1
        while 2 ** len(steps) < size:

            def move(place, reach=reach):
                at = place[low] + (0 if high is None else place[high] * self.sizes[low])
                at = (at + (reach if at % 2 else -reach)) % size
                place[low] = at % self.sizes[low]
                if high is not None:
                    place[high] = at // self.sizes[low]
                return place

            steps.append(self.pairs(move))
            reach = -2 * reach - 1
        return steps


def send(value, pairs):
    return lax.ppermute(value, AXES, pairs)


def once(step, value, turns):
    return lax.while_loop(
        lambda carry: carry[0] < turns,
        lambda carry: (carry[0] + 1, step(carry[1])),
        (jnp.int32(0), value),
    )[1]


def sum_over(value, steps):
    for pairs in steps:
        value = value + send(value, pairs)
    return value


def make_body(routes):
    text_pairs, image_pairs = routes.towers()
    y_pairs = routes.across_y()
    z_steps = routes.ring(1, 2)
    flat_steps = [routes.along(5, near), *routes.ring(None, 3), *routes.ring(4, 0)]
    early_steps, middle_steps = flat_steps[:4], flat_steps[4:] + z_steps[:-2]
    late_steps = z_steps[-2:]

    def body(image_feats, text_feats, gains, shifts, log_scale, logit_bias):
        scale = jnp.exp(log_scale)
        scalars = jnp.concatenate([scale, logit_bias])
        turns = jnp.where(log_scale[0] == log_scale[0], 1, 0)
        text = forward_norm(1, text_feats[0], gains, shifts)
        image = forward_norm(0, image_feats[0], gains, shifts)
        rows = image_feats.shape[1]

        text_z = send(text, text_pairs)
        text_y = send(text, y_pairs)
        image_late, text_z = lax.optimization_barrier((image, text_z))
        image_z = send(image_late, image_pairs)
        text_zy = once(lambda block: send(block, y_pairs), text_z, turns)
        texts = [text, text_z, text_y, text_zy]
        text_parts, image_part, loss_own, sums = tile(scalars, gains, shifts, image, texts)
        text_part, text_z_part, y_parts, image_z_part, sums = tile(
            scalars, gains, shifts, image_z, texts, [text_parts, sums]
        )

        image_back = send(image_z_part, image_pairs)
        y_back = send(y_parts, y_pairs)
        sums = once(lambda value: sum_over(value, early_steps), sums, turns)
        sums, y_back = lax.optimization_barrier((sums, y_back))
        text_z_sum = text_z_part + y_back[:rows].astype(jnp.float32)
        text_z_back = send(text_z_sum.astype(jnp.bfloat16), text_pairs)
        sums = once(lambda value: sum_over(value, middle_steps), sums, turns)
        sums, image_back, text_z_back = lax.optimization_barrier((sums, image_back, text_z_back))
        image_grad, row_mean = backward_norm(
            0,
            image_feats[0],
            gains,
            shifts,
            scale,
            [(0, image_part), (0, image_back)],
            loss_own,
        )
        sums = sums + send(sums, late_steps[0])
        sums, image_grad = lax.optimization_barrier((sums, image_grad))
        for pairs in late_steps[1:]:
            sums = sums + send(sums, pairs)
        (text_grad,) = backward_norm(
            1,
            text_feats[0],
            gains,
            shifts,
            scale,
            [(0, text_part), (rows, y_back), (0, text_z_back)],
        )
        return (image_grad[None], text_grad[None], sums[:2], sums[2:], row_mean)

    return body


def build(mesh, sizes):
    placed = (P("dp", "img", None), P("dp", "img", None), P(), P(), P(), P())
    return jax.shard_map(
        make_body(Routes(sizes)),
        mesh=mesh,
        in_specs=placed,
        out_specs=(P("dp", "img", None), P("dp", "img", None), P(), P(), P("dp", "img")),
        check_vma=False,
    )


def solution(mesh):
    y_high, cores = Y_HIGH, mesh.shape["dp"] // Y_HIGH
    y_low = mesh.shape["img"] // (RING * Z_BLOCK * X_CHIPS)
    return build(mesh, (y_low, RING, Z_BLOCK, X_CHIPS, y_high, cores))
```

```python
import functools

import jax
import jax.numpy as jnp
from jax import lax
from jax.experimental import pallas as pl
from jax.experimental.pallas import tpu as pltpu
from jax.sharding import PartitionSpec as P

AXES = ("img", "dp")
RING = 4
X_CHIPS = 4
Z_BLOCK = 4
Y_HIGH = 4

VMEM_LIMIT = 60 << 20
TILE_VMEM_LIMIT = 24 << 20
ROW_BLOCK = 16
UNROLL = 4
EPS = 1e-06
EXTRA = 8
LANES = 256
NT = (((1,), (1,)), ((), ()))
TN = (((0,), (0,)), ((), ()))


def to_lanes(column):
    count = column.shape[0]
    on = lax.broadcasted_iota(jnp.int32, (count, count), 0) == lax.broadcasted_iota(
        jnp.int32, (count, count), 1
    )
    return jnp.sum(jnp.where(on, column, 0.0), axis=0, keepdims=True)


def to_rows(line):
    count = line.shape[1]
    on = lax.broadcasted_iota(jnp.int32, (count, count), 0) == lax.broadcasted_iota(
        jnp.int32, (count, count), 1
    )
    return jnp.sum(jnp.where(on, line, 0.0), axis=1, keepdims=True)


def put_line(ref, line):
    count = line.shape[1]
    rows = ref.shape[0] - EXTRA
    ref[rows:, :] = jnp.zeros((EXTRA, ref.shape[1]), ref.dtype)
    for term in range(3):
        piece = line.astype(jnp.bfloat16)
        line = line - piece.astype(jnp.float32)
        ref[rows:, term * LANES : term * LANES + count] = jnp.broadcast_to(piece, (EXTRA, count))


def get_line(block, count):
    terms = [
        block[:1, term * LANES : term * LANES + count].astype(jnp.float32) for term in range(3)
    ]
    return terms[0] + (terms[1] + terms[2])


def norm_rows(feats, gain, shift):
    center = jnp.mean(feats, axis=-1, keepdims=True)
    offset = feats - center
    spread = jnp.mean(offset * offset, axis=-1, keepdims=True)
    rstd = lax.rsqrt(spread + EPS)
    normed = offset * rstd
    unnormed = normed * gain + shift
    inverse = lax.rsqrt(jnp.sum(unnormed * unnormed, axis=-1, keepdims=True) + EPS)
    return normed, rstd, unnormed, inverse


def forward_kernel(tower, feats_ref, gains_ref, shifts_ref, emb_ref, keep):
    gain = gains_ref[tower : tower + 1, :]
    shift = shifts_ref[tower : tower + 1, :]

    @pl.loop(0, feats_ref.shape[0] // ROW_BLOCK, unroll=UNROLL)
    def _(step):
        rows = pl.ds(pl.multiple_of(step * ROW_BLOCK, ROW_BLOCK), ROW_BLOCK)
        feats = feats_ref[rows, :].astype(jnp.float32)
        _, _, unnormed, inverse = norm_rows(feats, gain, shift)
        emb_ref[rows, :] = (unnormed * inverse).astype(jnp.bfloat16)
        keep[rows, :] = jnp.broadcast_to(inverse, (ROW_BLOCK, 128))

    put_line(emb_ref, to_lanes(keep[:, :1]))


def forward_norm(tower, feats, gains, shifts):
    rows, width = feats.shape
    return pl.pallas_call(
        functools.partial(forward_kernel, tower),
        out_shape=jax.ShapeDtypeStruct((rows + EXTRA, width), jnp.bfloat16),
        scratch_shapes=[pltpu.VMEM((rows, 128), jnp.float32)],
        compiler_params=pltpu.CompilerParams(vmem_limit_bytes=VMEM_LIMIT),
        cost_estimate=pl.CostEstimate(
            flops=20 * rows * width, bytes_accessed=4 * rows * width, transcendentals=0
        ),
        name="forward_norm",
    )(feats, gains, shifts)


def add_sums(units, parts, inverses):
    along = jnp.sum(units * parts, axis=-1, keepdims=True)
    pulled = parts - units * along
    return (
        jnp.sum(units * pulled, axis=0, keepdims=True),
        jnp.sum(inverses * pulled, axis=0, keepdims=True),
    )


def tile_kernel(final, scalars_ref, gains_ref, shifts_ref, *refs):
    image_in, text_ins = refs[0], refs[1:5]
    if final:
        parts_before, sums_before = refs[5:7]
        text_ref, text_z_ref, texts_ref, image_ref, sums_ref = refs[7:12]
    else:
        parts_ref, image_ref, loss_ref, sums_ref = refs[5:9]
    texts, coeff = refs[-2:]
    rows = coeff.shape[0]
    image = image_in[:rows, :]
    for at, ref in enumerate(text_ins):
        texts[at * rows : (at + 1) * rows, :] = ref[:rows, :]
    logits = lax.dot_general(image, texts[...], NT, preferred_element_type=jnp.float32)
    logits = scalars_ref[0] * logits + scalars_ref[1]
    if not final:
        row_at = lax.broadcasted_iota(jnp.int32, logits.shape, 0)
        column_at = lax.broadcasted_iota(jnp.int32, logits.shape, 1)
        signs = jnp.where(row_at == column_at, -1.0, 1.0)
        logits = signs * logits
    small = jnp.exp(-jnp.abs(logits))
    terms = jnp.maximum(logits, 0.0) + jnp.log1p(small)
    slopes = jnp.where(logits >= 0.0, 1.0, small) / (1.0 + small)
    if not final:
        slopes = signs * slopes
    coeff[...] = slopes.astype(jnp.bfloat16)
    losses = to_lanes(jnp.sum(terms, axis=1, keepdims=True))
    if final:
        put_line(image_ref, losses)
    else:
        loss_ref[...] = losses

    unit_sum, shift_sum = 0.0, 0.0
    for at in (3, 2, 1, 0):
        own = slice(at * rows, (at + 1) * rows)
        part = lax.dot_general(coeff[:, own], image, TN, preferred_element_type=jnp.float32)
        if not final:
            parts_ref[own, :] = part
        elif at >= 2:
            whole = part + parts_before[own, :]
            texts_ref[(3 - at) * rows : (4 - at) * rows, :] = whole.astype(jnp.bfloat16)
        else:
            (text_ref, text_z_ref)[at][...] = part + parts_before[own, :]
        inverse = to_rows(get_line(text_ins[at][rows:, :], rows))
        unit_add, shift_add = add_sums(texts[own, :].astype(jnp.float32), part, inverse)
        unit_sum, shift_sum = unit_sum + unit_add, shift_sum + shift_add
    part = jnp.dot(coeff[...], texts[...], preferred_element_type=jnp.float32)
    if final:
        image_ref[:rows, :] = part.astype(jnp.bfloat16)
    else:
        image_ref[...] = part
    inverse = to_rows(get_line(image_in[rows:, :], rows))
    image_unit_sum, image_shift_sum = add_sums(image.astype(jnp.float32), part, inverse)
    sums = (image_unit_sum, unit_sum, image_shift_sum, shift_sum)
    if not final:
        for at in range(4):
            sums_ref[at : at + 1, :] = sums[at]
        return
    for tower in range(2):
        shift = shifts_ref[tower : tower + 1, :]
        unit_sum = sums[tower] + sums_before[tower : tower + 1, :]
        shift_sum = sums[2 + tower] + sums_before[2 + tower : 3 + tower, :]
        gain_sum = (unit_sum - shift * shift_sum) / gains_ref[tower : tower + 1, :]
        sums_ref[tower : tower + 1, :] = scalars_ref[0] * gain_sum
        sums_ref[2 + tower : 3 + tower, :] = scalars_ref[0] * shift_sum


def tile(scalars, gains, shifts, image, texts, before=()):
    rows, width = image.shape[0] - EXTRA, image.shape[1]
    final = len(before) > 0
    whole = pl.BlockSpec(memory_space=pltpu.VMEM)

    def wide(count, kind):
        return jax.ShapeDtypeStruct((count, width), kind)

    if final:
        outs = [pltpu.HBM((rows, width), jnp.float32)] * 2
        outs += [wide(2 * rows, jnp.bfloat16), wide(rows + EXTRA, jnp.bfloat16)]
    else:
        outs = [wide(4 * rows, jnp.float32), pltpu.HBM((rows, width), jnp.float32)]
        outs += [jax.ShapeDtypeStruct((1, rows), jnp.float32)]
    outs += [wide(4, jnp.float32)]
    return pl.pallas_call(
        functools.partial(tile_kernel, final),
        out_shape=tuple(outs),
        in_specs=[pl.BlockSpec(memory_space=pltpu.SMEM)] + [whole] * (7 + len(before)),
        out_specs=(whole,) * len(outs),
        scratch_shapes=[
            pltpu.VMEM((4 * rows, width), jnp.bfloat16),
            pltpu.VMEM((rows, 4 * rows), jnp.bfloat16),
        ],
        compiler_params=pltpu.CompilerParams(vmem_limit_bytes=TILE_VMEM_LIMIT),
        cost_estimate=pl.CostEstimate(
            flops=24 * rows * rows * width,
            bytes_accessed=24 * rows * width,
            transcendentals=12 * rows * rows,
        ),
        name="last_tile" if final else "first_tile",
    )(scalars, gains, shifts, image, *texts, *before)


def backward_kernel(tower, firsts, feats_ref, gains_ref, shifts_ref, scale_ref, *refs):
    count = len(firsts)
    part_refs = refs[:count]
    if len(refs) > count + 1:
        loss_ref, grad_ref, mean_ref = refs[count:]
        rows = loss_ref.shape[1]
        losses = loss_ref[...] + get_line(part_refs[-1][rows:, :], rows)
        mean_ref[...] = losses / (2 * RING * rows)
    else:
        grad_ref = refs[count]

    @pl.loop(0, feats_ref.shape[0] // ROW_BLOCK, unroll=True)
    def _(step):
        rows = pl.ds(pl.multiple_of(step * ROW_BLOCK, ROW_BLOCK), ROW_BLOCK)
        feats = feats_ref[rows, :].astype(jnp.float32)
        gain = gains_ref[tower : tower + 1, :]
        shift = shifts_ref[tower : tower + 1, :]
        normed, rstd, unnormed, inverse = norm_rows(feats, gain, shift)
        unit = unnormed * inverse
        pulled = 0.0
        for first, part_ref in zip(firsts, part_refs):
            at = pl.ds(pl.multiple_of(first + step * ROW_BLOCK, ROW_BLOCK), ROW_BLOCK)
            pulled = pulled + part_ref[at, :].astype(jnp.float32)
        pulled = pulled * scale_ref[0]
        along = jnp.sum(unit * pulled, axis=-1, keepdims=True)
        pulled = inverse * (pulled - unit * along) * gain
        pulled = pulled - normed * jnp.mean(pulled * normed, axis=-1, keepdims=True)
        pulled = rstd * (pulled - jnp.mean(pulled, axis=-1, keepdims=True))
        grad_ref[rows, :] = pulled.astype(jnp.bfloat16)


def backward_norm(tower, feats, gains, shifts, scale, parts, loss=None):
    rows, width = feats.shape
    firsts = [first for first, _ in parts]
    values = [part for _, part in parts]
    whole = pl.BlockSpec(memory_space=pltpu.VMEM)
    out_shape = (jax.ShapeDtypeStruct((rows, width), jnp.bfloat16),)
    if loss is not None:
        values.append(loss)
        out_shape += (jax.ShapeDtypeStruct((1, rows), jnp.float32),)
    return pl.pallas_call(
        functools.partial(backward_kernel, tower, firsts),
        out_shape=out_shape,
        in_specs=[whole] * 3 + [pl.BlockSpec(memory_space=pltpu.SMEM)] + [whole] * len(values),
        out_specs=(whole,) * len(out_shape),
        compiler_params=pltpu.CompilerParams(vmem_limit_bytes=VMEM_LIMIT),
        cost_estimate=pl.CostEstimate(
            flops=40 * rows * width, bytes_accessed=12 * rows * width, transcendentals=0
        ),
        name="backward_norm",
    )(feats, gains, shifts, scale, *values)


def near(place):
    return place ^ 1


def far(place):
    return RING - 1 - place


class Routes:
    def __init__(self, sizes):
        self.sizes = sizes
        y_lo, z_hi, z_lo, x, y_hi, core = sizes
        self.count = y_lo * z_hi * z_lo * x * y_hi * core

    def split(self, index):
        place = []
        for size in reversed(self.sizes):
            place.append(index % size)
            index //= size
        return place[::-1]

    def join(self, place):
        index = 0
        for size, at in zip(self.sizes, place):
            index = index * size + at
        return index

    def pairs(self, move):
        out = []
        for index in range(self.count):
            place = self.split(index)
            out.append((index, self.join(move(list(place)))))
        return out

    def along(self, axis, step):
        def move(place):
            place[axis] = step(place[axis])
            return place

        return self.pairs(move)

    def across_y(self):
        return self.along(0, near)

    def towers(self):
        def text(place):
            place[1] = far(place[1]) if place[5] == 0 else near(place[1])
            return place

        def image(place):
            place[1] = near(place[1]) if place[5] == 0 else far(place[1])
            return place

        return self.pairs(text), self.pairs(image)

    def ring(self, high, low):
        size = self.sizes[low] * (1 if high is None else self.sizes[high])
        steps = []
        reach = -1
        while 2 ** len(steps) < size:

            def move(place, reach=reach):
                at = place[low] + (0 if high is None else place[high] * self.sizes[low])
                at = (at + (reach if at % 2 else -reach)) % size
                place[low] = at % self.sizes[low]
                if high is not None:
                    place[high] = at // self.sizes[low]
                return place

            steps.append(self.pairs(move))
            reach = -2 * reach - 1
        return steps


def send(value, pairs):
    return lax.ppermute(value, AXES, pairs)


def once(step, value, turns):
    return lax.while_loop(
        lambda carry: carry[0] < turns,
        lambda carry: (carry[0] + 1, step(carry[1])),
        (jnp.int32(0), value),
    )[1]


def sum_over(value, steps):
    for pairs in steps:
        value = value + send(value, pairs)
    return value


def make_body(routes):
    text_pairs, image_pairs = routes.towers()
    y_pairs = routes.across_y()
    z_steps = routes.ring(1, 2)
    flat_steps = [routes.along(5, near), *routes.ring(None, 3), *routes.ring(4, 0)]
    early_steps, middle_steps = flat_steps[:4], flat_steps[4:] + z_steps[:-2]
    late_steps = z_steps[-2:]

    def body(image_feats, text_feats, gains, shifts, log_scale, logit_bias):
        scale = jnp.exp(log_scale)
        scalars = jnp.concatenate([scale, logit_bias])
        turns = jnp.where(log_scale[0] == log_scale[0], 1, 0)
        text = forward_norm(1, text_feats[0], gains, shifts)
        image = forward_norm(0, image_feats[0], gains, shifts)
        rows = image_feats.shape[1]

        text_z = send(text, text_pairs)
        text_y = send(text, y_pairs)
        image_late, text_z = lax.optimization_barrier((image, text_z))
        image_z = send(image_late, image_pairs)
        text_zy = once(lambda block: send(block, y_pairs), text_z, turns)
        texts = [text, text_z, text_y, text_zy]
        text_parts, image_part, loss_own, sums = tile(scalars, gains, shifts, image, texts)
        text_part, text_z_part, y_parts, image_z_part, sums = tile(
            scalars, gains, shifts, image_z, texts, [text_parts, sums]
        )

        image_back = send(image_z_part, image_pairs)
        y_back = send(y_parts, y_pairs)
        sums = once(lambda value: sum_over(value, early_steps), sums, turns)
        sums, y_back = lax.optimization_barrier((sums, y_back))
        text_z_sum = text_z_part + y_back[:rows].astype(jnp.float32)
        text_z_back = send(text_z_sum.astype(jnp.bfloat16), text_pairs)
        sums = once(lambda value: sum_over(value, middle_steps), sums, turns)
        sums, image_back, text_z_back = lax.optimization_barrier((sums, image_back, text_z_back))
        image_grad, row_mean = backward_norm(
            0,
            image_feats[0],
            gains,
            shifts,
            scale,
            [(0, image_part), (0, image_back)],
            loss_own,
        )
        sums = sums + send(sums, late_steps[0])
        sums, image_grad = lax.optimization_barrier((sums, image_grad))
        for pairs in late_steps[1:]:
            sums = sums + send(sums, pairs)
        (text_grad,) = backward_norm(
            1,
            text_feats[0],
            gains,
            shifts,
            scale,
            [(0, text_part), (rows, y_back), (0, text_z_back)],
        )
        return (image_grad[None], text_grad[None], sums[:2], sums[2:], row_mean)

    return body


def build(mesh, sizes):
    placed = (P("dp", "img", None), P("dp", "img", None), P(), P(), P(), P())
    return jax.shard_map(
        make_body(Routes(sizes)),
        mesh=mesh,
        in_specs=placed,
        out_specs=(P("dp", "img", None), P("dp", "img", None), P(), P(), P("dp", "img")),
        check_vma=False,
    )


def solution(mesh):
    y_high, cores = Y_HIGH, mesh.shape["dp"] // Y_HIGH
    y_low = mesh.shape["img"] // (RING * Z_BLOCK * X_CHIPS)
    return build(mesh, (y_low, RING, Z_BLOCK, X_CHIPS, y_high, cores))
```
